32 devices in a mesh: slab: 8 (over z, y), pen: 4 (over x, core).
Axes of the slice: x: 2, y: 2, z: 4, core: 2. Of those that a mesh axis runs over, the one named last changes fastest.
Arguments:
- counts: int32 [256, 16], P('slab', 'pen'), may hold values from 0 to 512, as said below
- row_base: int32 [256, 16, 512], P('slab', 'pen'), may hold values from 0 to 15
- z_base: int32 [256, 16, 512], P('slab', 'pen'), may hold values from 0 to 255
- fractions: float32 [3, 256, 16, 512], P(None, 'slab', 'pen'), may hold values from 0 to 0.999
- strength: float32 [3, 256, 16, 512], P(None, 'slab', 'pen'), may hold values from -72 to 72
Outputs:
- vorticity: float32 [3, 256, 256, 256], P(None, 'slab', 'pen')
- velocity: float32 [3, 256, 256, 256], P(None, 'slab', 'pen')
- stretching: float32 [3, 256, 256, 256], P(None, 'slab', 'pen')
The draws below stay inside these ranges and needn't reach their ends.
Inputs may be any that keep to these rules, and one draw needn't show every extreme that they name: Slots s < counts[q, b] of group (q, b) hold particles, the others are unused; some group holds exactly 512 particles.
All inputs are finite; a program needn't handle non-finite values.
Results may differ from the reference program's by a relative error of at most 0.0052.
Values sent between devices are 32-bit elements; how exact they have to be, the bound alone decides.
No kernel may reach another device: no remote copies, remote signals or barrier semaphores. Data moves between devices by JAX's collectives and lax.ppermute only.
A program may use at most 192 MiB of HBM per device.

```python
import math
import jax
import jax.numpy as jnp
from jax import lax

NX = 256
NY = 256
NZ = 256
BLOCK_ROWS = 16
BLOCKS = 16
GC = 512


def draw_counts(key, part):
    fill_key = jax.random.fold_in(key, 11)
    plane_key = jax.random.fold_in(key, 12)
    spot_key = jax.random.fold_in(key, 13)
    filling = jax.random.randint(fill_key, (NX, BLOCKS), 1, GC + 1)
    plane_weight = jax.random.randint(plane_key, (NX, 1), 1, 5)
    result = filling * plane_weight // 4
    spot = jax.random.randint(spot_key, (), 0, NX * BLOCKS)
    flat_counts = result.reshape(-1)
    flat_counts = jnp.where(jnp.arange(NX * BLOCKS) == spot, GC, flat_counts)
    return flat_counts.reshape(NX, BLOCKS).astype(jnp.int32)


def place_ends(values, rng, smallest, largest):
    longest = values.shape.index(max(values.shape))
    spots = []
    for shift in (0, 1):
        where = [jax.random.randint(jax.random.fold_in(rng, axis), (), 0, length) for axis, length in enumerate(values.shape)]
        where[longest] = (where[longest] + shift) % values.shape[longest]
        spots.append(tuple(where))
    return values.at[spots[0]].set(smallest).at[spots[1]].set(largest)


def block_levels(own_key, dims, shards, low, top_value):
    loudness = 1.0
    for axis_at, parts in shards:
        steps = jax.random.uniform(jax.random.fold_in(jax.random.fold_in(own_key, 6), axis_at), (parts,), jnp.float32, low / len(shards), top_value / len(shards))
        loudness = loudness * jnp.repeat(jnp.exp(steps), dims[axis_at] // parts).reshape((-1,) + (1,) * (len(dims) - 1 - axis_at))
    return loudness


def scatter_about(stream_key, extent, scale, reach, split=(), held_as=jnp.bfloat16):
    entries = jax.random.normal(stream_key, extent, jnp.float32) * scale
    if len(split) > 0:
        entries = block_levels(stream_key, extent, split, -0.22, 0.18) * entries
    return jnp.clip(entries, min=-reach, max=reach).astype(held_as)


def setup_inputs(seed: int = 0) -> dict:
    key_of = jax.random.split(jax.random.key(seed), 6)
    return {
        "counts": draw_counts(jax.random.fold_in(key_of[5], 71), 0),
        "row_base": place_ends(jax.random.randint(key_of[1], (NX, BLOCKS, GC), 0, BLOCK_ROWS), jax.random.fold_in(key_of[1], 1), 0, BLOCK_ROWS - 1).astype(jnp.int32),
        "z_base": place_ends(jax.random.randint(key_of[2], (NX, BLOCKS, GC), 0, NZ), jax.random.fold_in(key_of[2], 1), 0, NZ - 1).astype(jnp.int32),
        "fractions": jnp.clip(0.999 * jax.random.uniform(key_of[3], (3, NX, BLOCKS, GC), jnp.float32) ** block_levels(key_of[3], (3, NX, BLOCKS, GC), ((1, 8), (2, 4)), -0.2, 0.2), 0.0, 0.999),
        "strength": scatter_about(key_of[4], (3, NX, BLOCKS, GC), 12.0, 72.0, ((1, 8), (2, 4)), jnp.float32),
    }


def kernel_weight(distance):
    magnitude = jnp.abs(distance)
    inner_part = 1.0 - 2.5 * magnitude * magnitude + 1.5 * magnitude * magnitude * magnitude
    outer_part = 0.5 * (2.0 - magnitude) * (2.0 - magnitude) * (1.0 - magnitude)
    return jnp.where(magnitude < 1.0, inner_part, jnp.where(magnitude < 2.0, outer_part, 0.0))


def wavenumbers(frequency, length):
    signed_index = jnp.where(frequency < length // 2, frequency, frequency - length)
    full_wave = (2.0 * math.pi / length) * signed_index.astype(jnp.float32)
    curl_wave = jnp.where(frequency == length // 2, 0.0, full_wave)
    return full_wave, curl_wave


def central(values, axis):
    return (8.0 * (jnp.roll(values, -1, axis) - jnp.roll(values, 1, axis)) - (jnp.roll(values, -2, axis) - jnp.roll(values, 2, axis))) / 12.0


def reference(counts, row_base, z_base, fractions, strength):
    slot_index = jnp.arange(GC, dtype=jnp.int32)
    active = (slot_index[None, None, :] < counts[:, :, None]).astype(jnp.float32)
    plane_index = jnp.arange(NX, dtype=jnp.int32)[:, None, None]
    block_start = (BLOCK_ROWS * jnp.arange(BLOCKS, dtype=jnp.int32))[None, :, None]
    row_start = block_start + row_base
    vorticity = jnp.zeros((3, NX * NY * NZ), jnp.float32)
    for shift_x in range(4):
        weight_x = kernel_weight((shift_x - 1) - fractions[0])
        for shift_y in range(4):
            weight_y = kernel_weight((shift_y - 1) - fractions[1])
            coefs = ((strength * weight_x) * weight_y * active).astype(jnp.bfloat16)
            coefs = lax.optimization_barrier(coefs).astype(jnp.float32)
            x_cells = (plane_index + shift_x) % NX
            y_cells = (row_start + shift_y) % NY
            for shift_z in range(4):
                weight_z = kernel_weight((shift_z - 1) - fractions[2]).astype(jnp.bfloat16)
                weight_z = lax.optimization_barrier(weight_z).astype(jnp.float32)
                z_cells = (z_base + shift_z) % NZ
                flat_index = ((x_cells * NY + y_cells) * NZ + z_cells).reshape(-1).astype(jnp.int32)
                vorticity = vorticity.at[:, flat_index].add((coefs * weight_z).reshape(3, -1))
    vorticity = vorticity.reshape(3, NX, NY, NZ)
    spectrum = jnp.fft.fftn(vorticity, axes=(1, 2, 3))
    full_x, curl_x = wavenumbers(jnp.arange(NX, dtype=jnp.int32), NX)
    full_y, curl_y = wavenumbers(jnp.arange(NY, dtype=jnp.int32), NY)
    full_z, curl_z = wavenumbers(jnp.arange(NZ, dtype=jnp.int32), NZ)
    full_x, curl_x = full_x[:, None, None], curl_x[:, None, None]
    full_y, curl_y = full_y[None, :, None], curl_y[None, :, None]
    full_z, curl_z = full_z[None, None, :], curl_z[None, None, :]
    wave_squared = full_x * full_x + full_y * full_y + full_z * full_z
    scaling = jnp.where(wave_squared > 0.0, 1.0 / jnp.where(wave_squared > 0.0, wave_squared, 1.0), 0.0)
    cross_first = curl_y * spectrum[2] - curl_z * spectrum[1]
    cross_second = curl_z * spectrum[0] - curl_x * spectrum[2]
    cross_third = curl_x * spectrum[1] - curl_y * spectrum[0]
    velocity_spectrum = 1j * jnp.stack([cross_first, cross_second, cross_third]) * scaling
    velocity = jnp.real(jnp.fft.ifftn(velocity_spectrum, axes=(1, 2, 3))).astype(jnp.float32)
    rows_out = []
    for component in range(3):
        total = vorticity[0] * central(velocity[component], 0)
        total = total + vorticity[1] * central(velocity[component], 1)
        total = total + vorticity[2] * central(velocity[component], 2)
        rows_out.append(total)
    stretching = jnp.stack(rows_out)
    return vorticity, velocity, stretching
```

```python
import functools
import math

import jax
import jax.numpy as jnp
import numpy as np
from jax import lax
from jax.experimental import pallas as pl
from jax.experimental.pallas import tpu as pltpu
from jax.sharding import PartitionSpec as P

NZ = 256
BLOCK_ROWS = 16
HALF = NZ // 2
STEP = 8
SLOTS_AT_ONCE = 256
MIB = 1024 * 1024
ORDER = (1, 2, 0)
AXES = ("slab", "pen")


def kernel_weight(distance):
    magnitude = jnp.abs(distance)
    inner_part = 1.0 - 2.5 * magnitude * magnitude + 1.5 * magnitude * magnitude * magnitude
    outer_part = 0.5 * (2.0 - magnitude) * (2.0 - magnitude) * (1.0 - magnitude)
    return jnp.where(magnitude < 1.0, inner_part, jnp.where(magnitude < 2.0, outer_part, 0.0))


def vmem(limit=48, **extra):
    return pltpu.CompilerParams(vmem_limit_bytes=limit * MIB, **extra)


def cost(flops, moved):
    return pl.CostEstimate(flops=int(flops), bytes_accessed=int(moved), transcendentals=0)


def two_parts(table):
    table = np.asarray(table, np.float32)
    high = table.astype(jnp.bfloat16)
    low = (table - high.astype(np.float32)).astype(jnp.bfloat16)
    return high, low


def right_table(table):
    high, low = two_parts(table)
    return jnp.asarray(np.concatenate([high, high, low], axis=0))


def left_table(table):
    high, low = two_parts(table)
    return jnp.asarray(np.concatenate([high, high, low], axis=1))


def waves(length):
    index = np.arange(length)
    angle = 2.0 * np.pi / length * (index[:, None] * index[None, :] % length)
    return np.cos(angle), np.sin(angle)


def z_forward_table():
    cosine, sine = waves(NZ)
    real_part, imaginary = cosine[:, :HALF].copy(), -sine[:, :HALF]
    imaginary[:, 0] = cosine[:, HALF]
    return np.concatenate([real_part, imaginary], axis=1)


def z_inverse_table():
    cosine, sine = waves(NZ)
    real_part, imaginary = 2.0 * cosine[:HALF], -2.0 * sine[:HALF]
    real_part[0] = 1.0
    imaginary[0] = cosine[HALF]
    return np.concatenate([real_part, imaginary], axis=0)


def y_forward_table(length, parts):
    cosine, sine = waves(length)
    width = length // parts
    rows = []
    for part in range(parts):
        here = slice(part * width, (part + 1) * width)
        rows.append(np.concatenate([cosine[here], -sine[here]], axis=1))
        rows.append(np.concatenate([sine[here], cosine[here]], axis=1))
    return np.concatenate(rows, axis=0)


def y_inverse_table(length, parts):
    cosine, sine = waves(length)
    width = length // parts
    columns = []
    for part in range(parts):
        here = slice(part * width, (part + 1) * width)
        columns.append(np.concatenate([cosine[:, here], -sine[:, here]], axis=0))
        columns.append(np.concatenate([sine[:, here], cosine[:, here]], axis=0))
    return np.concatenate(columns, axis=1)


def x_table(length, sign):
    cosine, sine = waves(length)
    return np.concatenate(
        [
            np.concatenate([cosine, -sign * sine], axis=1),
            np.concatenate([sign * sine, cosine], axis=1),
        ],
        axis=0,
    )


def split_values(values):
    high = values.astype(jnp.bfloat16)
    low = (values - high.astype(jnp.float32)).astype(jnp.bfloat16)
    return high, low


def times_right(values, table):
    high, low = split_values(values)
    return jnp.dot(
        jnp.concatenate([high, low, high], axis=1), table, preferred_element_type=jnp.float32
    )


def times_left(table, values):
    high, low = split_values(values)
    return jnp.dot(
        table, jnp.concatenate([high, low, high], axis=0), preferred_element_type=jnp.float32
    )


def deposit_kernel(
    counts, row_base, z_base, fractions, strength, grid, ghost_x, ghost_y, ghost_xy, rows
):
    planes, blocks, slots = row_base.shape
    width = min(SLOTS_AT_ONCE, slots)
    rows_local = blocks * BLOCK_ROWS
    ext = BLOCK_ROWS + 8

    def clear(plane, _):
        grid[:, plane] = jnp.zeros((3,) + grid.shape[2:], jnp.float32)
        return 0

    lax.fori_loop(0, planes + 3, clear, 0)
    z_rows = 16
    z_iota = lax.broadcasted_iota(jnp.int32, (z_rows, width), 0)
    j_iota = lax.broadcasted_iota(jnp.int32, (ext, width), 0).astype(jnp.float32)
    z_tiles = [(z_iota + z_rows * t).astype(jnp.float32).astype(jnp.bfloat16) for t in range(NZ // z_rows)]

    def one_plane(plane, _):
        slot = lax.broadcasted_iota(jnp.int32, (blocks, slots), 1)
        group = lax.broadcasted_iota(jnp.int32, (blocks, slots), 0)
        count = jnp.zeros((blocks, slots), jnp.int32)
        for block in range(blocks):
            count = jnp.where(group == block, counts[plane, block], count)
        live = slot < count
        row_cell = row_base[plane].astype(jnp.float32)
        z_cell = z_base[plane]
        for offset in range(4):
            weight_x = kernel_weight(float(offset - 1) - fractions[0, plane])
            for part in range(3):
                rows[part * 4 + offset] = jnp.where(live, strength[part, plane] * weight_x, 0.0)
            rows[12 + offset] = kernel_weight(float(offset - 1) - fractions[1, plane])
            rows[16 + offset] = row_cell + float(offset)
            rows[20 + offset] = kernel_weight(float(offset - 1) - fractions[2, plane])
            rows[24 + offset] = jnp.bitwise_and(z_cell + offset, NZ - 1).astype(jnp.float32)

        def spread(block, first):
            here = slice(first, first + width)

            def row(index):
                return rows[index, block : block + 1, here]

            weight_y = jnp.zeros((ext, width), jnp.float32)
            for offset in range(4):
                weight_y = jnp.where(j_iota == row(16 + offset), row(12 + offset), weight_y)
            coefs = jnp.concatenate([row(index) * weight_y for index in range(12)], axis=0)
            coefs = coefs.astype(jnp.bfloat16)
            z_weight = [
                jnp.broadcast_to(row(20 + offset), (z_rows, width)).astype(jnp.bfloat16)
                for offset in range(4)
            ]
            z_place = [
                jnp.broadcast_to(row(24 + offset), (z_rows, width)).astype(jnp.bfloat16)
                for offset in range(4)
            ]
            tiles = []
            for z_tile in z_tiles:
                tile = jnp.zeros((z_rows, width), jnp.bfloat16)
                for offset in range(4):
                    tile = jnp.where(z_tile == z_place[offset], z_weight[offset], tile)
                tiles.append(tile)
            weight_z = jnp.concatenate(tiles, axis=0)
            result = lax.dot_general(
                coefs, weight_z, (((1,), (1,)), ((), ())), preferred_element_type=jnp.float32
            )
            low = block * BLOCK_ROWS
            for part in range(3):
                for offset in range(4):
                    index = part * 4 + offset
                    grid[part, plane + offset, low : low + ext, :] += result[
                        index * ext : (index + 1) * ext
                    ]

        for block in range(blocks):
            spread(block, 0)
        for first in range(width, slots, width):
            for block in range(blocks):
                pl.when(counts[plane, block] > first)(functools.partial(spread, block, first))
        return 0

    lax.fori_loop(0, planes, one_plane, 0)
    for part in range(3):
        for offset in range(3):
            ghost_x[part, offset] = grid[part, planes + offset, :rows_local, :]
            ghost_xy[part, offset] = grid[part, planes + offset, rows_local : rows_local + 3, :]

    def side(plane, _):
        ghost_y[:, plane] = grid[:, plane, rows_local : rows_local + 3, :]
        return 0

    lax.fori_loop(0, planes, side, 0)


def deposit(counts, row_base, z_base, fractions, strength):
    planes, blocks, slots = row_base.shape
    rows_local = blocks * BLOCK_ROWS
    whole = pl.BlockSpec(memory_space=pltpu.VMEM)
    return pl.pallas_call(
        deposit_kernel,
        out_shape=(
            jax.ShapeDtypeStruct((3, planes + 3, rows_local + 8, NZ), jnp.float32),
            jax.ShapeDtypeStruct((3, 3, rows_local, NZ), jnp.float32),
            jax.ShapeDtypeStruct((3, planes, 3, NZ), jnp.float32),
            jax.ShapeDtypeStruct((3, 3, 3, NZ), jnp.float32),
        ),
        in_specs=[pl.BlockSpec(memory_space=pltpu.SMEM)] + [whole] * 4,
        out_specs=(whole,) * 4,
        scratch_shapes=[
            pltpu.VMEM((28, blocks, slots), jnp.float32),
        ],
        compiler_params=vmem(),
        cost_estimate=cost(2 * planes * blocks * 288 * slots * NZ, 12 * MIB),
        name="deposit",
    )(counts, row_base, z_base, fractions, strength)


def next_over(block, axes):
    counts = [lax.axis_size(axis) for axis in AXES]
    route = []
    for slab in range(counts[0]):
        for pen in range(counts[1]):
            to_slab = (slab + 1) % counts[0] if "slab" in axes else slab
            to_pen = (pen + 1) % counts[1] if "pen" in axes else pen
            route.append((slab * counts[1] + pen, to_slab * counts[1] + to_pen))
    return lax.ppermute(block, AXES, route)


def shifted(block, axis, distance):
    count = lax.axis_size(axis)
    return lax.ppermute(block, axis, [(i, (i + distance) % count) for i in range(count)])


def z_forward_kernel(grid, ghost_x, ghost_y, ghost_xy, table, *refs):
    vorticity, send = refs[-2:]
    rows_local = vorticity.shape[2]
    vorticity[0] = grid[0, :, :rows_local, :]
    vorticity[0, :, 0:3, :] += ghost_y[0]

    @pl.when(pl.program_id(0) == 0)
    def _():
        vorticity[0, 0:3] += ghost_x[0]
        vorticity[0, 0:3, 0:3, :] += ghost_xy[0]

    spectrum = times_right(vorticity[0].reshape(STEP * rows_local, NZ), table[...])
    lines = send.reshape(HALF * STEP, 2 * rows_local)
    for plane in range(STEP):
        here = spectrum[plane * rows_local : (plane + 1) * rows_local]
        stacked = jnp.concatenate([here[:, :HALF], here[:, HALF:]], axis=0)
        lines[pl.ds(plane, HALF, stride=STEP), :] = stacked.T


def z_forward(part, grid, ghosts, vorticity, devices):
    ghost_x, ghost_y, ghost_xy = ghosts
    planes = ghost_y.shape[1]
    rows_local = ghost_x.shape[2]
    depth = HALF // devices
    table = right_table(z_forward_table())
    specs = [
        pl.BlockSpec((1, STEP, rows_local + 8, NZ), lambda i: (part, i, 0, 0)),
        pl.BlockSpec((1, 3, rows_local, NZ), lambda i: (part, 0, 0, 0)),
        pl.BlockSpec((1, STEP, 3, NZ), lambda i: (part, i, 0, 0)),
        pl.BlockSpec((1, 3, 3, NZ), lambda i: (part, 0, 0, 0)),
        pl.BlockSpec(table.shape, lambda i: (0, 0)),
    ]
    operands = [grid, ghost_x, ghost_y, ghost_xy, table]
    aliases = {}
    if vorticity is not None:
        aliases = {len(operands): 0}
        specs.append(pl.BlockSpec(memory_space=pl.ANY))
        operands.append(vorticity)
    return pl.pallas_call(
        z_forward_kernel,
        grid=(planes // STEP,),
        in_specs=specs,
        out_specs=(
            pl.BlockSpec((1, STEP, rows_local, NZ), lambda i: (part, i, 0, 0)),
            pl.BlockSpec((devices, depth, STEP, 2 * rows_local), lambda i: (0, 0, i, 0)),
        ),
        out_shape=(
            jax.ShapeDtypeStruct((3, planes, rows_local, NZ), jnp.float32),
            jax.ShapeDtypeStruct((devices, depth, planes, 2 * rows_local), jnp.float32),
        ),
        input_output_aliases=aliases,
        compiler_params=vmem(),
        cost_estimate=cost(6 * planes * rows_local * NZ * NZ, 3 * planes * rows_local * NZ * 4),
        name="z_forward",
    )(*operands)


def z_inverse_kernel(received, table, velocity, low_x, high_x, low_y, high_y):
    rows_local = velocity.shape[1]
    lines = received.reshape(HALF * STEP, 2 * rows_local)
    pieces = []
    for plane in range(STEP):
        turned = lines[pl.ds(plane, HALF, stride=STEP), :].T
        pieces.append(jnp.concatenate([turned[:rows_local], turned[rows_local:]], axis=1))
    values = times_right(jnp.concatenate(pieces, axis=0), table[...])
    velocity[...] = values.reshape(STEP, rows_local, NZ)
    low_y[...] = velocity[:, 0:2, :]
    high_y[...] = velocity[:, rows_local - 2 : rows_local, :]

    @pl.when(pl.program_id(0) == 0)
    def _():
        low_x[...] = velocity[0:2]

    @pl.when(pl.program_id(0) == pl.num_programs(0) - 1)
    def _():
        high_x[...] = velocity[STEP - 2 : STEP]


def z_inverse(received):
    devices, depth, planes, width = received.shape
    rows_local = width // 2
    table = right_table(z_inverse_table())
    layer = pl.BlockSpec((2, rows_local, NZ), lambda i: (0, 0, 0))
    edge = pl.BlockSpec((STEP, 2, NZ), lambda i: (i, 0, 0))
    return pl.pallas_call(
        z_inverse_kernel,
        grid=(planes // STEP,),
        in_specs=[
            pl.BlockSpec((devices, depth, STEP, width), lambda i: (0, 0, i, 0)),
            pl.BlockSpec(table.shape, lambda i: (0, 0)),
        ],
        out_specs=(
            pl.BlockSpec((STEP, rows_local, NZ), lambda i: (i, 0, 0)),
            layer,
            layer,
            edge,
            edge,
        ),
        out_shape=(
            jax.ShapeDtypeStruct((planes, rows_local, NZ), jnp.float32),
            jax.ShapeDtypeStruct((2, rows_local, NZ), jnp.float32),
            jax.ShapeDtypeStruct((2, rows_local, NZ), jnp.float32),
            jax.ShapeDtypeStruct((planes, 2, NZ), jnp.float32),
            jax.ShapeDtypeStruct((planes, 2, NZ), jnp.float32),
        ),
        compiler_params=vmem(),
        cost_estimate=cost(6 * planes * rows_local * NZ * NZ, 2 * planes * rows_local * NZ * 4),
        name="z_inverse",
    )(received, table)


def plane_forward_kernel(start, received, y_table, x_table_ref, spectrum):
    step = pl.program_id(0)
    depth = pl.num_programs(0) - 1
    has_first = start[0] == 0

    @pl.when(jnp.logical_or(step < depth, has_first))
    def _():
        slabs, pens, _, planes, width = received.shape
        pieces = [received[:, pen, 0].reshape(slabs * planes, width) for pen in range(pens)]
        lane = lax.broadcasted_iota(jnp.int32, (1, width), 1)
        real_side = lane < width // 2
        keep_real = jnp.logical_or(real_side, jnp.logical_not(jnp.logical_and(has_first, step == 0)))
        keep_imaginary = jnp.logical_or(jnp.logical_not(real_side), step < depth)
        keep = jnp.logical_and(keep_real, keep_imaginary).astype(jnp.float32)
        lines = jnp.concatenate([piece * keep for piece in pieces], axis=1)
        along_y = times_right(lines, y_table[...])
        rows_y = along_y.shape[1] // 2
        stacked = jnp.concatenate([along_y[:, :rows_y], along_y[:, rows_y:]], axis=0)
        spectrum[0] = times_left(x_table_ref[...], stacked)


def plane_forward(start, received):
    slabs, pens, depth, planes, width = received.shape
    size_x = slabs * planes
    size_y = pens * (width // 2)
    y_table = right_table(y_forward_table(size_y, pens))
    x_matrix = left_table(x_table(size_x, -1.0))
    return pl.pallas_call(
        plane_forward_kernel,
        grid=(depth + 1,),
        in_specs=[
            pl.BlockSpec(memory_space=pltpu.SMEM),
            pl.BlockSpec(
                (slabs, pens, 1, planes, width), lambda j: (0, 0, jnp.where(j < depth, j, 0), 0, 0)
            ),
            pl.BlockSpec(y_table.shape, lambda j: (0, 0)),
            pl.BlockSpec(x_matrix.shape, lambda j: (0, 0)),
        ],
        out_specs=pl.BlockSpec((1, 2 * size_x, size_y), lambda j: (j, 0, 0)),
        out_shape=jax.ShapeDtypeStruct((depth + 1, 2 * size_x, size_y), jnp.float32),
        compiler_params=vmem(),
        cost_estimate=cost(
            24 * depth * size_x * size_y * (size_x + size_y), 4 * depth * size_x * size_y * 4
        ),
        name="plane_forward",
    )(start, received, y_table, x_matrix)


def wave_pair(shape, dim, length):
    index = lax.broadcasted_iota(jnp.int32, shape, dim)
    signed_index = jnp.where(index < length // 2, index, index - length)
    full_wave = (2.0 * math.pi / length) * signed_index.astype(jnp.float32)
    return full_wave, jnp.where(index == length // 2, 0.0, full_wave)


def plane_inverse_kernel(
    part, start, first, second, first_extra, second_extra, y_table, x_table_ref, back, turned
):
    step = pl.program_id(0)
    size_y = first.shape[2]
    size_x = first.shape[1] // 2
    full_x, curl_x = wave_pair((size_x, 1), 0, size_x)
    full_y, curl_y = wave_pair((1, size_y), 1, size_y)

    def curl(left, right, full_z, curl_z):
        curls = (curl_x, curl_y, curl_z)
        wave_left, wave_right = curls[(part + 1) % 3], curls[(part + 2) % 3]
        wave_squared = full_x * full_x + full_y * full_y + full_z * full_z
        present = wave_squared > 0.0
        scaling = jnp.where(present, 1.0 / jnp.where(present, wave_squared, 1.0), 0.0)
        scaling = scaling * (1.0 / float(size_x * size_y * NZ))
        real_part = wave_left * right[0, :size_x] - wave_right * left[0, :size_x]
        imaginary = wave_left * right[0, size_x:] - wave_right * left[0, size_x:]
        return -imaginary * scaling, real_part * scaling

    index_z = (start[0] + step).astype(jnp.float32)
    wave_z = (2.0 * math.pi / NZ) * index_z
    real_part, imaginary = curl(first, second, wave_z, wave_z)
    turned[:size_x] = real_part
    turned[size_x:] = imaginary

    @pl.when(jnp.logical_and(start[0] == 0, step == 0))
    def _():
        extra_real, extra_imaginary = curl(first_extra, second_extra, -math.pi, 0.0)
        turned[:size_x] += extra_real
        turned[size_x:] += extra_imaginary

    along_x = times_left(x_table_ref[...], turned[...])
    lines = jnp.concatenate([along_x[:size_x], along_x[size_x:]], axis=1)
    result = times_right(lines, y_table[...])
    slabs, pens, _, planes, width = back.shape
    for pen in range(pens):
        back[:, pen, 0] = result[:, pen * width : (pen + 1) * width].reshape(slabs, planes, width)


def plane_inverse(part, start, first, second, shape):
    slabs, pens, depth, planes, width = shape
    size_x = slabs * planes
    size_y = pens * (width // 2)
    y_table = right_table(y_inverse_table(size_y, pens))
    x_matrix = left_table(x_table(size_x, 1.0))
    now = pl.BlockSpec((1, 2 * size_x, size_y), lambda j: (j, 0, 0))
    extra = pl.BlockSpec((1, 2 * size_x, size_y), lambda j: (depth, 0, 0))
    return pl.pallas_call(
        functools.partial(plane_inverse_kernel, part),
        grid=(depth,),
        in_specs=[
            pl.BlockSpec(memory_space=pltpu.SMEM),
            now,
            now,
            extra,
            extra,
            pl.BlockSpec(y_table.shape, lambda j: (0, 0)),
            pl.BlockSpec(x_matrix.shape, lambda j: (0, 0)),
        ],
        out_specs=pl.BlockSpec((slabs, pens, 1, planes, width), lambda j: (0, 0, j, 0, 0)),
        out_shape=jax.ShapeDtypeStruct(shape, jnp.float32),
        scratch_shapes=[pltpu.VMEM((2 * size_x, size_y), jnp.float32)],
        compiler_params=vmem(),
        cost_estimate=cost(
            24 * depth * size_x * size_y * (size_x + size_y), 6 * depth * size_x * size_y * 4
        ),
        name="plane_inverse",
    )(start, first, second, first, second, y_table, x_matrix)


def stretch_kernel(vorticity, field, low_x, high_x, low_y, high_y, *refs):
    velocity, stretching, padded = refs[-3:]
    step = pl.program_id(0)
    planes, rows_local, _ = field.shape

    @pl.when(step == 0)
    def _():
        padded[0:2, 8 : 8 + rows_local, :] = low_x[...]
        padded[planes + 2 : planes + 4, 8 : 8 + rows_local, :] = high_x[...]

        def fill(plane, _):
            padded[plane + 2, 8 : 8 + rows_local, :] = field[plane]
            padded[plane + 2, 6:8, :] = low_y[plane]
            padded[plane + 2, 8 + rows_local : 10 + rows_local, :] = high_y[plane]
            return 0

        lax.fori_loop(0, planes, fill, 0)

    own = slice(8, 8 + rows_local)

    def difference(ahead, behind, ahead_2, behind_2):
        return (2.0 / 3.0) * (ahead - behind) - (1.0 / 12.0) * (ahead_2 - behind_2)

    def one(plane, _):
        at = step * STEP + plane + 2
        here = padded[at, own, :]
        along_x = difference(
            padded[at + 1, own, :], padded[at - 1, own, :], padded[at + 2, own, :], padded[at - 2, own, :]
        )
        along_y = difference(
            *(padded[at, 8 + shift : 8 + shift + rows_local, :] for shift in (1, -1, 2, -2))
        )
        along_z = difference(*(pltpu.roll(here, shift % NZ, 1) for shift in (-1, 1, -2, 2)))
        velocity[0, plane] = here
        stretching[0, plane] = (
            vorticity[0, plane] * along_x + vorticity[1, plane] * along_y + vorticity[2, plane] * along_z
        )
        return 0

    lax.fori_loop(0, STEP, one, 0)


def stretch(part, vorticity, field, halos, outputs):
    planes, rows_local, _ = field.shape
    specs = [
        pl.BlockSpec((3, STEP, rows_local, NZ), lambda i: (0, i, 0, 0)),
        pl.BlockSpec(field.shape, lambda i: (0, 0, 0)),
    ] + [pl.BlockSpec(halo.shape, lambda i: (0, 0, 0)) for halo in halos]
    operands = [vorticity, field, *halos]
    aliases = {}
    if outputs is not None:
        aliases = {len(operands): 0, len(operands) + 1: 1}
        specs += [pl.BlockSpec(memory_space=pl.ANY)] * 2
        operands += list(outputs)
    shape = jax.ShapeDtypeStruct((3, planes, rows_local, NZ), jnp.float32)
    block = pl.BlockSpec((1, STEP, rows_local, NZ), lambda i: (part, i, 0, 0))
    return pl.pallas_call(
        stretch_kernel,
        grid=(planes // STEP,),
        in_specs=specs,
        out_specs=(block, block),
        out_shape=(shape, shape),
        input_output_aliases=aliases,
        scratch_shapes=[pltpu.VMEM((planes + 4, rows_local + 16, NZ), jnp.float32)],
        compiler_params=vmem(),
        cost_estimate=cost(20 * planes * rows_local * NZ, 6 * planes * rows_local * NZ * 4),
        name="stretch",
    )(*operands)


def per_device(counts, row_base, z_base, fractions, strength):
    slabs, pens = lax.axis_size("slab"), lax.axis_size("pen")
    devices = slabs * pens
    depth = HALF // devices
    planes, blocks, _ = row_base.shape
    rows_local = blocks * BLOCK_ROWS
    shape = (slabs, pens, depth, planes, 2 * rows_local)
    place = lax.axis_index("slab") * pens + lax.axis_index("pen")
    start = (place * depth).astype(jnp.int32).reshape(1)

    grid, ghost_x, ghost_y, ghost_xy = deposit(counts, row_base, z_base, fractions, strength)
    ghosts = (
        next_over(ghost_x, ("slab",)),
        next_over(ghost_y, ("pen",)),
        next_over(ghost_xy, ("slab", "pen")),
    )

    def exchange(blocks_out):
        flat = blocks_out.reshape(devices, depth, planes, 2 * rows_local)
        return lax.all_to_all(flat, AXES, 0, 0, tiled=True)

    vorticity = None
    spectra = {}
    for part in ORDER:
        vorticity, send = z_forward(part, grid, ghosts, vorticity, devices)
        spectra[part] = plane_forward(start, exchange(send).reshape(shape))

    outputs = None
    for part in (0, 1, 2):
        back = plane_inverse(part, start, spectra[(part + 1) % 3], spectra[(part + 2) % 3], shape)
        field, low_x, high_x, low_y, high_y = z_inverse(exchange(back))
        halos = (
            shifted(high_x, "slab", 1),
            shifted(low_x, "slab", -1),
            shifted(high_y, "pen", 1),
            shifted(low_y, "pen", -1),
        )
        outputs = stretch(part, vorticity, field, halos, outputs)
    return (vorticity, outputs[0], outputs[1])


def solution(mesh):
    in_specs = (
        P("slab", "pen"),
        P("slab", "pen", None),
        P("slab", "pen", None),
        P(None, "slab", "pen", None),
        P(None, "slab", "pen", None),
    )
    out_specs = (
        P(None, "slab", "pen", None),
        P(None, "slab", "pen", None),
        P(None, "slab", "pen", None),
    )
    return jax.shard_map(
        per_device, mesh=mesh, in_specs=in_specs, out_specs=out_specs, check_vma=False
    )
```

```python
import functools
import math

import jax
import jax.numpy as jnp
import numpy as np
from jax import lax
from jax.experimental import pallas as pl
from jax.experimental.pallas import tpu as pltpu
from jax.sharding import PartitionSpec as P

NZ = 256
BLOCK_ROWS = 16
HALF = NZ // 2
STEP = 8
SLOTS_AT_ONCE = 256
MIB = 1024 * 1024
FORWARD = ((1, 2), (0,))
BACKWARD = ((0,), (1, 2))
AXES = ("slab", "pen")


def kernel_weight(distance):
    magnitude = jnp.abs(distance)
    inner_part = 1.0 - 2.5 * magnitude * magnitude + 1.5 * magnitude * magnitude * magnitude
    outer_part = 0.5 * (2.0 - magnitude) * (2.0 - magnitude) * (1.0 - magnitude)
    return jnp.where(magnitude < 1.0, inner_part, jnp.where(magnitude < 2.0, outer_part, 0.0))


def vmem(limit=48, **extra):
    return pltpu.CompilerParams(vmem_limit_bytes=limit * MIB, **extra)


def cost(flops, moved):
    return pl.CostEstimate(flops=int(flops), bytes_accessed=int(moved), transcendentals=0)


def two_parts(table):
    table = np.asarray(table, np.float32)
    high = table.astype(jnp.bfloat16)
    low = (table - high.astype(np.float32)).astype(jnp.bfloat16)
    return high, low


def right_table(table):
    high, low = two_parts(table)
    return jnp.asarray(np.concatenate([high, high, low], axis=0))


def left_table(table):
    high, low = two_parts(table)
    return jnp.asarray(np.concatenate([high, high, low], axis=1))


def waves(length):
    index = np.arange(length)
    angle = 2.0 * np.pi / length * (index[:, None] * index[None, :] % length)
    return np.cos(angle), np.sin(angle)


def z_forward_table():
    cosine, sine = waves(NZ)
    real_part, imaginary = cosine[:, :HALF].copy(), -sine[:, :HALF]
    imaginary[:, 0] = cosine[:, HALF]
    return np.concatenate([real_part, imaginary], axis=1)


def z_inverse_table():
    cosine, sine = waves(NZ)
    real_part, imaginary = 2.0 * cosine[:HALF], -2.0 * sine[:HALF]
    real_part[0] = 1.0
    imaginary[0] = cosine[HALF]
    return np.concatenate([real_part, imaginary], axis=0)


def y_forward_table(length, parts):
    cosine, sine = waves(length)
    width = length // parts
    rows = []
    for part in range(parts):
        here = slice(part * width, (part + 1) * width)
        rows.append(np.concatenate([cosine[here], -sine[here]], axis=1))
        rows.append(np.concatenate([sine[here], cosine[here]], axis=1))
    return np.concatenate(rows, axis=0)


def y_inverse_table(length, parts):
    cosine, sine = waves(length)
    width = length // parts
    columns = []
    for part in range(parts):
        here = slice(part * width, (part + 1) * width)
        columns.append(np.concatenate([cosine[:, here], -sine[:, here]], axis=0))
        columns.append(np.concatenate([sine[:, here], cosine[:, here]], axis=0))
    return np.concatenate(columns, axis=1)


def x_table(length, sign):
    cosine, sine = waves(length)
    return np.concatenate(
        [
            np.concatenate([cosine, -sign * sine], axis=1),
            np.concatenate([sign * sine, cosine], axis=1),
        ],
        axis=0,
    )


def split_values(values):
    high = values.astype(jnp.bfloat16)
    low = (values - high.astype(jnp.float32)).astype(jnp.bfloat16)
    return high, low


def times_right(values, table):
    high, low = split_values(values)
    return jnp.dot(
        jnp.concatenate([high, low, high], axis=1), table, preferred_element_type=jnp.float32
    )


def times_left(table, values):
    high, low = split_values(values)
    return jnp.dot(
        table, jnp.concatenate([high, low, high], axis=0), preferred_element_type=jnp.float32
    )


def deposit_plan(edges, planes, blocks):
    edge_planes = range(planes - 3, planes)
    if edges:
        return ((0, planes - 3, (blocks - 1,)), (edge_planes[0], planes, tuple(range(blocks))))
    return ((0, planes - 3, tuple(range(blocks - 1))),)


def deposit_kernel(edges, counts, row_base, z_base, fractions, strength, *refs):
    planes, blocks, slots = row_base.shape
    width = min(SLOTS_AT_ONCE, slots)
    rows_local = blocks * BLOCK_ROWS
    ext = BLOCK_ROWS + 8
    if edges:
        grid, ghost_x, ghost_y, ghost_xy, rows = refs
    else:
        begun, grid, rows = refs

    def clear(plane, _):
        if edges:
            grid[:, plane] = jnp.zeros((3,) + grid.shape[2:], jnp.float32)
        else:
            grid[:, plane] = begun[:, plane]
        return 0

    lax.fori_loop(0, grid.shape[1], clear, 0)
    z_rows = 16
    z_iota = lax.broadcasted_iota(jnp.int32, (z_rows, width), 0)
    j_iota = lax.broadcasted_iota(jnp.int32, (ext, width), 0).astype(jnp.float32)
    z_tiles = [
        (z_iota + z_rows * t).astype(jnp.float32).astype(jnp.bfloat16) for t in range(NZ // z_rows)
    ]

    def one_plane(here_blocks, plane, _):
        slot = lax.broadcasted_iota(jnp.int32, (blocks, slots), 1)
        group = lax.broadcasted_iota(jnp.int32, (blocks, slots), 0)
        count = jnp.zeros((blocks, slots), jnp.int32)
        for block in here_blocks:
            count = jnp.where(group == block, counts[plane, block], count)
        live = slot < count
        row_cell = row_base[plane].astype(jnp.float32)
        z_cell = z_base[plane]
        for offset in range(4):
            weight_x = kernel_weight(float(offset - 1) - fractions[0, plane])
            for part in range(3):
                rows[part * 4 + offset] = jnp.where(live, strength[part, plane] * weight_x, 0.0)
            rows[12 + offset] = kernel_weight(float(offset - 1) - fractions[1, plane])
            rows[16 + offset] = row_cell + float(offset)
            rows[20 + offset] = kernel_weight(float(offset - 1) - fractions[2, plane])
            rows[24 + offset] = jnp.bitwise_and(z_cell + offset, NZ - 1).astype(jnp.float32)

        def spread(block, first):
            here = slice(first, first + width)

            def row(index):
                return rows[index, block : block + 1, here]

            weight_y = jnp.zeros((ext, width), jnp.float32)
            for offset in range(4):
                weight_y = jnp.where(j_iota == row(16 + offset), row(12 + offset), weight_y)
            coefs = jnp.concatenate([row(index) * weight_y for index in range(12)], axis=0)
            coefs = coefs.astype(jnp.bfloat16)
            z_weight = [
                jnp.broadcast_to(row(20 + offset), (z_rows, width)).astype(jnp.bfloat16)
                for offset in range(4)
            ]
            z_place = [
                jnp.broadcast_to(row(24 + offset), (z_rows, width)).astype(jnp.bfloat16)
                for offset in range(4)
            ]
            tiles = []
            for z_tile in z_tiles:
                tile = jnp.zeros((z_rows, width), jnp.bfloat16)
                for offset in range(4):
                    tile = jnp.where(z_tile == z_place[offset], z_weight[offset], tile)
                tiles.append(tile)
            weight_z = jnp.concatenate(tiles, axis=0)
            result = lax.dot_general(
                coefs, weight_z, (((1,), (1,)), ((), ())), preferred_element_type=jnp.float32
            )
            low = block * BLOCK_ROWS
            for part in range(3):
                for offset in range(4):
                    index = part * 4 + offset
                    grid[part, plane + offset, low : low + ext, :] += result[
                        index * ext : (index + 1) * ext
                    ]

        for block in here_blocks:
            spread(block, 0)
        for first in range(width, slots, width):
            for block in here_blocks:
                pl.when(counts[plane, block] > first)(functools.partial(spread, block, first))
        return 0

    for begin, end, here_blocks in deposit_plan(edges, planes, blocks):
        if here_blocks:
            lax.fori_loop(begin, end, functools.partial(one_plane, here_blocks), 0)
    if not edges:
        return
    for part in range(3):
        for offset in range(3):
            ghost_x[part, offset] = grid[part, planes + offset, :rows_local, :]
            ghost_xy[part, offset] = grid[part, planes + offset, rows_local : rows_local + 3, :]

    def side(plane, _):
        ghost_y[:, plane] = grid[:, plane, rows_local : rows_local + 3, :]
        return 0

    lax.fori_loop(0, planes, side, 0)


def deposit(particles, begun):
    edges = begun is None
    planes, blocks, slots = particles[1].shape
    rows_local = blocks * BLOCK_ROWS
    whole = pl.BlockSpec(memory_space=pltpu.VMEM)
    grid_shape = (3, planes + 3, rows_local + 8, NZ)
    shapes = [grid_shape]
    if edges:
        shapes += [(3, 3, rows_local, NZ), (3, planes, 3, NZ), (3, 3, 3, NZ)]
    groups = sum((end - begin) * len(here) for begin, end, here in deposit_plan(edges, planes, blocks))
    operands = list(particles) + ([] if edges else [begun])
    return pl.pallas_call(
        functools.partial(deposit_kernel, edges),
        out_shape=[jax.ShapeDtypeStruct(shape, jnp.float32) for shape in shapes],
        in_specs=[pl.BlockSpec(memory_space=pltpu.SMEM)] + [whole] * (len(operands) - 1),
        out_specs=[whole] * len(shapes),
        scratch_shapes=[pltpu.VMEM((28, blocks, slots), jnp.float32)],
        compiler_params=vmem(),
        cost_estimate=cost(10 * groups * 288 * slots * NZ, 12 * MIB),
        name="deposit_edges" if edges else "deposit_rest",
    )(*operands)


def next_over(block, axes):
    counts = [lax.axis_size(axis) for axis in AXES]
    route = []
    for slab in range(counts[0]):
        for pen in range(counts[1]):
            to_slab = (slab + 1) % counts[0] if "slab" in axes else slab
            to_pen = (pen + 1) % counts[1] if "pen" in axes else pen
            route.append((slab * counts[1] + pen, to_slab * counts[1] + to_pen))
    return lax.ppermute(block, AXES, route)


def shifted(block, axis, distance):
    count = lax.axis_size(axis)
    return lax.ppermute(block, axis, [(i, (i + distance) % count) for i in range(count)])


def z_forward_kernel(grid, ghost_x, ghost_y, ghost_xy, table, *refs):
    vorticity, send = refs[-2:]
    rows_local = vorticity.shape[2]
    vorticity[0] = grid[0, :, :rows_local, :]
    vorticity[0, :, 0:3, :] += ghost_y[0]

    @pl.when(pl.program_id(1) == 0)
    def _():
        vorticity[0, 0:3] += ghost_x[0]
        vorticity[0, 0:3, 0:3, :] += ghost_xy[0]

    spectrum = times_right(vorticity[0].reshape(STEP * rows_local, NZ), table[...])
    lines = send.reshape(HALF * STEP, 2 * rows_local)
    for plane in range(STEP):
        here = spectrum[plane * rows_local : (plane + 1) * rows_local]
        stacked = jnp.concatenate([here[:, :HALF], here[:, HALF:]], axis=0)
        lines[pl.ds(plane, HALF, stride=STEP), :] = stacked.T


def z_forward(parts, grid, ghosts, vorticity, devices):
    ghost_x, ghost_y, ghost_xy = ghosts
    planes = ghost_y.shape[1]
    rows_local = ghost_x.shape[2]
    depth = HALF // devices
    count = len(parts)
    part = parts[0]
    table = right_table(z_forward_table())
    specs = [
        pl.BlockSpec((1, STEP, rows_local + 8, NZ), lambda c, i: (part + c, i, 0, 0)),
        pl.BlockSpec((1, 3, rows_local, NZ), lambda c, i: (part + c, 0, 0, 0)),
        pl.BlockSpec((1, STEP, 3, NZ), lambda c, i: (part + c, i, 0, 0)),
        pl.BlockSpec((1, 3, 3, NZ), lambda c, i: (part + c, 0, 0, 0)),
        pl.BlockSpec(table.shape, lambda c, i: (0, 0)),
    ]
    operands = [grid, ghost_x, ghost_y, ghost_xy, table]
    aliases = {}
    if vorticity is not None:
        aliases = {len(operands): 0}
        specs.append(pl.BlockSpec(memory_space=pl.ANY))
        operands.append(vorticity)
    return pl.pallas_call(
        z_forward_kernel,
        grid=(count, planes // STEP),
        in_specs=specs,
        out_specs=(
            pl.BlockSpec((1, STEP, rows_local, NZ), lambda c, i: (part + c, i, 0, 0)),
            pl.BlockSpec((devices, None, depth, STEP, 2 * rows_local), lambda c, i: (0, c, 0, i, 0)),
        ),
        out_shape=(
            jax.ShapeDtypeStruct((3, planes, rows_local, NZ), jnp.float32),
            jax.ShapeDtypeStruct((devices, count, depth, planes, 2 * rows_local), jnp.float32),
        ),
        input_output_aliases=aliases,
        compiler_params=vmem(),
        cost_estimate=cost(
            6 * count * planes * rows_local * NZ * NZ, 3 * count * planes * rows_local * NZ * 4
        ),
        name="z_forward",
    )(*operands)


def z_inverse_kernel(received, table, *refs):
    velocity, low_x, high_x, low_y, high_y = refs[-5:]
    rows_local = velocity.shape[2]
    lines = received.reshape(HALF * STEP, 2 * rows_local)
    pieces = []
    for plane in range(STEP):
        turned = lines[pl.ds(plane, HALF, stride=STEP), :].T
        pieces.append(jnp.concatenate([turned[:rows_local], turned[rows_local:]], axis=1))
    values = times_right(jnp.concatenate(pieces, axis=0), table[...])
    velocity[0] = values.reshape(STEP, rows_local, NZ)
    low_y[0] = velocity[0, :, 0:2, :]
    high_y[0] = velocity[0, :, rows_local - 2 : rows_local, :]

    @pl.when(pl.program_id(1) == 0)
    def _():
        low_x[0] = velocity[0, 0:2]

    @pl.when(pl.program_id(1) == pl.num_programs(1) - 1)
    def _():
        high_x[0] = velocity[0, STEP - 2 : STEP]


def z_inverse(parts, received, velocity):
    devices, count, depth, planes, width = received.shape
    rows_local = width // 2
    part = parts[0]
    table = right_table(z_inverse_table())
    layer = pl.BlockSpec((1, 2, rows_local, NZ), lambda c, i: (c, 0, 0, 0))
    edge = pl.BlockSpec((1, STEP, 2, NZ), lambda c, i: (c, i, 0, 0))
    specs = [
        pl.BlockSpec((devices, None, depth, STEP, width), lambda c, i: (0, c, 0, i, 0)),
        pl.BlockSpec(table.shape, lambda c, i: (0, 0)),
    ]
    operands = [received, table]
    aliases = {}
    if velocity is not None:
        aliases = {len(operands): 0}
        specs.append(pl.BlockSpec(memory_space=pl.ANY))
        operands.append(velocity)
    return pl.pallas_call(
        z_inverse_kernel,
        grid=(count, planes // STEP),
        in_specs=specs,
        out_specs=(
            pl.BlockSpec((1, STEP, rows_local, NZ), lambda c, i: (part + c, i, 0, 0)),
            layer,
            layer,
            edge,
            edge,
        ),
        out_shape=(
            jax.ShapeDtypeStruct((3, planes, rows_local, NZ), jnp.float32),
            jax.ShapeDtypeStruct((count, 2, rows_local, NZ), jnp.float32),
            jax.ShapeDtypeStruct((count, 2, rows_local, NZ), jnp.float32),
            jax.ShapeDtypeStruct((count, planes, 2, NZ), jnp.float32),
            jax.ShapeDtypeStruct((count, planes, 2, NZ), jnp.float32),
        ),
        input_output_aliases=aliases,
        compiler_params=vmem(),
        cost_estimate=cost(
            6 * count * planes * rows_local * NZ * NZ, 2 * count * planes * rows_local * NZ * 4
        ),
        name="z_inverse",
    )(*operands)


def plane_forward_kernel(start, received, y_table, x_table_ref, spectrum):
    step = pl.program_id(1)
    depth = pl.num_programs(1) - 1
    has_first = start[0] == 0

    @pl.when(jnp.logical_or(step < depth, has_first))
    def _():
        slabs, pens, planes, width = received.shape
        pieces = [received[:, pen].reshape(slabs * planes, width) for pen in range(pens)]
        lane = lax.broadcasted_iota(jnp.int32, (1, width), 1)
        real_side = lane < width // 2
        keep_real = jnp.logical_or(real_side, jnp.logical_not(jnp.logical_and(has_first, step == 0)))
        keep_imaginary = jnp.logical_or(jnp.logical_not(real_side), step < depth)
        keep = jnp.logical_and(keep_real, keep_imaginary).astype(jnp.float32)
        lines = jnp.concatenate([piece * keep for piece in pieces], axis=1)
        along_y = times_right(lines, y_table[...])
        rows_y = along_y.shape[1] // 2
        stacked = jnp.concatenate([along_y[:, :rows_y], along_y[:, rows_y:]], axis=0)
        spectrum[...] = times_left(x_table_ref[...], stacked)


def plane_forward(start, received):
    slabs, pens, count, depth, planes, width = received.shape
    size_x = slabs * planes
    size_y = pens * (width // 2)
    y_table = right_table(y_forward_table(size_y, pens))
    x_matrix = left_table(x_table(size_x, -1.0))
    return pl.pallas_call(
        plane_forward_kernel,
        grid=(count, depth + 1),
        in_specs=[
            pl.BlockSpec(memory_space=pltpu.SMEM),
            pl.BlockSpec(
                (slabs, pens, None, None, planes, width),
                lambda c, j: (0, 0, c, jnp.where(j < depth, j, 0), 0, 0),
            ),
            pl.BlockSpec(y_table.shape, lambda c, j: (0, 0)),
            pl.BlockSpec(x_matrix.shape, lambda c, j: (0, 0)),
        ],
        out_specs=pl.BlockSpec((None, None, 2 * size_x, size_y), lambda c, j: (c, j, 0, 0)),
        out_shape=jax.ShapeDtypeStruct((count, depth + 1, 2 * size_x, size_y), jnp.float32),
        compiler_params=vmem(),
        cost_estimate=cost(
            24 * count * depth * size_x * size_y * (size_x + size_y),
            4 * count * depth * size_x * size_y * 4,
        ),
        name="plane_forward",
    )(start, received, y_table, x_matrix)


def wave_pair(shape, dim, length):
    index = lax.broadcasted_iota(jnp.int32, shape, dim)
    signed_index = jnp.where(index < length // 2, index, index - length)
    full_wave = (2.0 * math.pi / length) * signed_index.astype(jnp.float32)
    return full_wave, jnp.where(index == length // 2, 0.0, full_wave)


def plane_inverse_kernel(parts, needs, start, *refs):
    spectra = dict(zip(needs, refs[: len(needs)]))
    extras = dict(zip(needs, refs[len(needs) : 2 * len(needs)]))
    y_table, x_table_ref, back, turned = refs[2 * len(needs) :]
    step = pl.program_id(0)
    size_x, size_y = turned.shape[1] // 2, turned.shape[2]
    full_x, curl_x = wave_pair((size_x, 1), 0, size_x)
    full_y, curl_y = wave_pair((1, size_y), 1, size_y)

    def curl(part, source, full_z, curl_z):
        curls = (curl_x, curl_y, curl_z)
        wave_left, wave_right = curls[(part + 1) % 3], curls[(part + 2) % 3]
        left, right = source[(part + 1) % 3], source[(part + 2) % 3]
        wave_squared = full_x * full_x + full_y * full_y + full_z * full_z
        present = wave_squared > 0.0
        scaling = jnp.where(present, 1.0 / jnp.where(present, wave_squared, 1.0), 0.0)
        scaling = scaling * (1.0 / float(size_x * size_y * NZ))
        real_part = wave_left * right[:size_x] - wave_right * left[:size_x]
        imaginary = wave_left * right[size_x:] - wave_right * left[size_x:]
        return -imaginary * scaling, real_part * scaling

    index_z = (start[0] + step).astype(jnp.float32)
    wave_z = (2.0 * math.pi / NZ) * index_z
    for at, part in enumerate(parts):
        real_part, imaginary = curl(part, spectra, wave_z, wave_z)
        turned[at, :size_x] = real_part
        turned[at, size_x:] = imaginary

    @pl.when(jnp.logical_and(start[0] == 0, step == 0))
    def _():
        for at, part in enumerate(parts):
            extra_real, extra_imaginary = curl(part, extras, -math.pi, 0.0)
            turned[at, :size_x] += extra_real
            turned[at, size_x:] += extra_imaginary

    slabs, pens, _, planes, width = back.shape
    for at in range(len(parts)):
        along_x = times_left(x_table_ref[...], turned[at])
        lines = jnp.concatenate([along_x[:size_x], along_x[size_x:]], axis=1)
        result = times_right(lines, y_table[...])
        for pen in range(pens):
            piece = result[:, pen * width : (pen + 1) * width]
            back[:, pen, at] = piece.reshape(slabs, planes, width)


def plane_inverse(parts, start, spectra, shape):
    slabs, pens, depth, planes, width = shape
    count = len(parts)
    size_x = slabs * planes
    size_y = pens * (width // 2)
    y_table = right_table(y_inverse_table(size_y, pens))
    x_matrix = left_table(x_table(size_x, 1.0))
    needs = [c for c in range(3) if any(c != part for part in parts)]

    def at(index, extra):
        return pl.BlockSpec(
            (None, None, 2 * size_x, size_y),
            lambda j: (index, depth if extra else j, 0, 0),
        )

    return pl.pallas_call(
        functools.partial(plane_inverse_kernel, parts, needs),
        grid=(depth,),
        in_specs=[pl.BlockSpec(memory_space=pltpu.SMEM)]
        + [at(spectra[c][1], False) for c in needs]
        + [at(spectra[c][1], True) for c in needs]
        + [
            pl.BlockSpec(y_table.shape, lambda j: (0, 0)),
            pl.BlockSpec(x_matrix.shape, lambda j: (0, 0)),
        ],
        out_specs=pl.BlockSpec(
            (slabs, pens, count, None, planes, width), lambda j: (0, 0, 0, j, 0, 0)
        ),
        out_shape=jax.ShapeDtypeStruct((slabs, pens, count, depth, planes, width), jnp.float32),
        scratch_shapes=[pltpu.VMEM((count, 2 * size_x, size_y), jnp.float32)],
        compiler_params=vmem(),
        cost_estimate=cost(
            24 * count * depth * size_x * size_y * (size_x + size_y),
            6 * count * depth * size_x * size_y * 4,
        ),
        name="plane_inverse",
    )(start, *([spectra[c][0] for c in needs] * 2), y_table, x_matrix)


def stretch_kernel(vorticity, field, before, after, low_x, high_x, low_y, high_y, *refs):
    stretching, padded = refs[-2:]
    step = pl.program_id(0)
    rows_local = field.shape[2]
    first = step == 0
    last = step == pl.num_programs(0) - 1
    own = slice(8, 8 + rows_local)
    for plane in range(STEP):
        padded[plane, own, :] = field[0, plane]
        padded[plane, 6:8, :] = low_y[0, plane]
        padded[plane, 8 + rows_local : 10 + rows_local, :] = high_y[0, plane]

    def difference(ahead, behind, ahead_2, behind_2):
        return (2.0 / 3.0) * (ahead - behind) - (1.0 / 12.0) * (ahead_2 - behind_2)

    def along(plane):
        if plane < 0:
            return jnp.where(first, low_x[0, plane + 2], before[0, plane + 2])
        if plane >= STEP:
            return jnp.where(last, high_x[0, plane - STEP], after[0, plane - STEP])
        return field[0, plane]

    for plane in range(STEP):
        here = field[0, plane]
        along_x = difference(*(along(plane + shift) for shift in (1, -1, 2, -2)))
        along_y = difference(
            *(padded[plane, 8 + shift : 8 + shift + rows_local, :] for shift in (1, -1, 2, -2))
        )
        along_z = difference(*(pltpu.roll(here, shift % NZ, 1) for shift in (-1, 1, -2, 2)))
        stretching[0, plane] = (
            vorticity[0, plane] * along_x + vorticity[1, plane] * along_y + vorticity[2, plane] * along_z
        )


def stretch(parts, vorticity, velocity, halos, stretching):
    _, planes, rows_local, _ = velocity.shape
    part = parts[0]
    count = len(parts)
    pairs = STEP // 2
    low_x, high_x, low_y, high_y = halos
    layer = pl.BlockSpec((1, 2, rows_local, NZ), lambda i, c: (c, 0, 0, 0))
    edge = pl.BlockSpec((1, STEP, 2, NZ), lambda i, c: (c, i, 0, 0))
    block = pl.BlockSpec((1, STEP, rows_local, NZ), lambda i, c: (part + c, i, 0, 0))
    specs = [
        pl.BlockSpec((3, STEP, rows_local, NZ), lambda i, c: (0, i, 0, 0)),
        block,
        pl.BlockSpec(
            (1, 2, rows_local, NZ), lambda i, c: (part + c, jnp.maximum(i * pairs - 1, 0), 0, 0)
        ),
        pl.BlockSpec(
            (1, 2, rows_local, NZ),
            lambda i, c: (part + c, jnp.minimum((i + 1) * pairs, planes // 2 - 1), 0, 0),
        ),
        layer,
        layer,
        edge,
        edge,
    ]
    operands = [vorticity, velocity, velocity, velocity, *halos]
    aliases = {}
    if stretching is not None:
        aliases = {len(operands): 0}
        specs.append(pl.BlockSpec(memory_space=pl.ANY))
        operands.append(stretching)
    return pl.pallas_call(
        stretch_kernel,
        grid=(planes // STEP, count),
        in_specs=specs,
        out_specs=block,
        out_shape=jax.ShapeDtypeStruct((3, planes, rows_local, NZ), jnp.float32),
        input_output_aliases=aliases,
        scratch_shapes=[pltpu.VMEM((STEP, rows_local + 16, NZ), jnp.float32)],
        compiler_params=vmem(),
        cost_estimate=cost(
            40 * count * planes * rows_local * NZ, (3 + 3 * count) * planes * rows_local * NZ * 4
        ),
        name="stretch",
    )(*operands)


def per_device(counts, row_base, z_base, fractions, strength):
    slabs, pens = lax.axis_size("slab"), lax.axis_size("pen")
    devices = slabs * pens
    depth = HALF // devices
    planes, blocks, _ = row_base.shape
    rows_local = blocks * BLOCK_ROWS
    width = 2 * rows_local
    place = lax.axis_index("slab") * pens + lax.axis_index("pen")
    start = (place * depth).astype(jnp.int32).reshape(1)

    particles = (counts, row_base, z_base, fractions, strength)
    begun, ghost_x, ghost_y, ghost_xy = deposit(particles, None)
    ghosts = (
        next_over(ghost_x, ("slab",)),
        next_over(ghost_y, ("pen",)),
        next_over(ghost_xy, ("slab", "pen")),
    )
    (grid,) = deposit(particles, begun)

    def exchange(blocks_out):
        return lax.all_to_all(blocks_out, AXES, 0, 0, tiled=True)

    vorticity = received = None
    spectra = {}
    for parts in FORWARD:
        vorticity, send = z_forward(parts, grid, ghosts, vorticity, devices)
        if received is not None:
            send, _ = lax.optimization_barrier((send, received))
        received = exchange(send)
        spectrum = plane_forward(
            start, received.reshape(slabs, pens, len(parts), depth, planes, width)
        )
        for index, part in enumerate(parts):
            spectra[part] = (spectrum, index)

    velocity = stretching = None
    for parts in BACKWARD:
        back = plane_inverse(parts, start, spectra, (slabs, pens, depth, planes, width))
        received = exchange(back.reshape(devices, len(parts), depth, planes, width))
        if stretching is not None:
            received, stretching = lax.optimization_barrier((received, stretching))
        velocity, low_x, high_x, low_y, high_y = z_inverse(parts, received, velocity)
        halos = (
            shifted(high_x, "slab", 1),
            shifted(low_x, "slab", -1),
            shifted(high_y, "pen", 1),
            shifted(low_y, "pen", -1),
        )
        stretching = stretch(parts, vorticity, velocity, halos, stretching)
    return (vorticity, velocity, stretching)


def solution(mesh):
    in_specs = (
        P("slab", "pen"),
        P("slab", "pen", None),
        P("slab", "pen", None),
        P(None, "slab", "pen", None),
        P(None, "slab", "pen", None),
    )
    out_specs = (
        P(None, "slab", "pen", None),
        P(None, "slab", "pen", None),
        P(None, "slab", "pen", None),
    )
    return jax.shard_map(
        per_device, mesh=mesh, in_specs=in_specs, out_specs=out_specs, check_vma=False
    )
```

```python
import functools
import math

import jax
import jax.numpy as jnp
import numpy as np
from jax import lax
from jax.experimental import pallas as pl
from jax.experimental.pallas import tpu as pltpu
from jax.sharding import PartitionSpec as P

NZ = 256
BLOCK_ROWS = 16
HALF = NZ // 2
STEP = 8
SLOTS_AT_ONCE = 256
MIB = 1024 * 1024
NEW = object()
AXES = ("slab", "pen")


def kernel_weight(distance):
    magnitude = jnp.abs(distance)
    inner_part = 1.0 - 2.5 * magnitude * magnitude + 1.5 * magnitude * magnitude * magnitude
    outer_part = 0.5 * (2.0 - magnitude) * (2.0 - magnitude) * (1.0 - magnitude)
    return jnp.where(magnitude < 1.0, inner_part, jnp.where(magnitude < 2.0, outer_part, 0.0))


def vmem(limit=48, **extra):
    return pltpu.CompilerParams(vmem_limit_bytes=limit * MIB, **extra)


def cost(flops, moved):
    return pl.CostEstimate(flops=int(flops), bytes_accessed=int(moved), transcendentals=0)


def two_parts(table):
    table = np.asarray(table, np.float32)
    high = table.astype(jnp.bfloat16)
    low = (table - high.astype(np.float32)).astype(jnp.bfloat16)
    return high, low


def right_table(table):
    high, low = two_parts(table)
    return jnp.asarray(np.concatenate([high, high, low], axis=0))


def left_table(table):
    high, low = two_parts(table)
    return jnp.asarray(np.concatenate([high, high, low], axis=1))


def waves(length):
    index = np.arange(length)
    angle = 2.0 * np.pi / length * (index[:, None] * index[None, :] % length)
    return np.cos(angle), np.sin(angle)


def z_forward_table():
    cosine, sine = waves(NZ)
    real_part, imaginary = cosine[:, :HALF].copy(), -sine[:, :HALF]
    imaginary[:, 0] = cosine[:, HALF]
    return np.concatenate([real_part, imaginary], axis=1)


def z_inverse_table():
    cosine, sine = waves(NZ)
    real_part, imaginary = 2.0 * cosine[:HALF], -2.0 * sine[:HALF]
    real_part[0] = 1.0
    imaginary[0] = cosine[HALF]
    return np.concatenate([real_part, imaginary], axis=0)


def y_forward_table(length, parts):
    cosine, sine = waves(length)
    width = length // parts
    rows = []
    for part in range(parts):
        here = slice(part * width, (part + 1) * width)
        rows.append(np.concatenate([cosine[here], -sine[here]], axis=1))
        rows.append(np.concatenate([sine[here], cosine[here]], axis=1))
    return np.concatenate(rows, axis=0)


def y_inverse_table(length, parts):
    cosine, sine = waves(length)
    width = length // parts
    columns = []
    for part in range(parts):
        here = slice(part * width, (part + 1) * width)
        columns.append(np.concatenate([cosine[:, here], -sine[:, here]], axis=0))
        columns.append(np.concatenate([sine[:, here], cosine[:, here]], axis=0))
    return np.concatenate(columns, axis=1)


def x_table(length, sign):
    cosine, sine = waves(length)
    return np.concatenate(
        [
            np.concatenate([cosine, -sign * sine], axis=1),
            np.concatenate([sign * sine, cosine], axis=1),
        ],
        axis=0,
    )


def split_values(values):
    high = values.astype(jnp.bfloat16)
    low = (values - high.astype(jnp.float32)).astype(jnp.bfloat16)
    return high, low


def times_right(values, table):
    high, low = split_values(values)
    return jnp.dot(
        jnp.concatenate([high, low, high], axis=1), table, preferred_element_type=jnp.float32
    )


def times_left(table, values):
    high, low = split_values(values)
    return jnp.dot(
        table, jnp.concatenate([high, low, high], axis=0), preferred_element_type=jnp.float32
    )


def deposit_kernel(begin, end, counts, row_base, z_base, fractions, strength, *refs):
    planes, blocks, slots = row_base.shape
    first_source = max(begin - 3, 0)
    last = end == planes
    width = min(SLOTS_AT_ONCE, slots)
    rows_local = blocks * BLOCK_ROWS
    ext = BLOCK_ROWS + 8
    if last:
        grid, ghost_y, ghost_x, ghost_xy = refs[:4]
    else:
        grid, ghost_y = refs[:2]
    rows, row_here, z_here, fractions_here, strength_here, arrived = refs[-6:]
    taken = slice(first_source, end)
    copies = [
        pltpu.make_async_copy(row_base.at[taken], row_here, arrived.at[0]),
        pltpu.make_async_copy(z_base.at[taken], z_here, arrived.at[1]),
        pltpu.make_async_copy(fractions.at[:, taken], fractions_here, arrived.at[2]),
        pltpu.make_async_copy(strength.at[:, taken], strength_here, arrived.at[3]),
    ]
    for copy in copies:
        copy.start()

    def clear(plane, _):
        grid[:, plane] = jnp.zeros((3,) + grid.shape[2:], jnp.float32)
        return 0

    lax.fori_loop(0, grid.shape[1], clear, 0)
    z_rows = 16
    z_iota = lax.broadcasted_iota(jnp.int32, (z_rows, width), 0)
    j_iota = lax.broadcasted_iota(jnp.int32, (ext, width), 0).astype(jnp.float32)
    z_tiles = [
        (z_iota + z_rows * t).astype(jnp.float32).astype(jnp.bfloat16) for t in range(NZ // z_rows)
    ]
    for copy in copies:
        copy.wait()

    def one_plane(offsets, source, _):
        plane = source + first_source
        slot = lax.broadcasted_iota(jnp.int32, (blocks, slots), 1)
        group = lax.broadcasted_iota(jnp.int32, (blocks, slots), 0)
        count = jnp.zeros((blocks, slots), jnp.int32)
        for block in range(blocks):
            count = jnp.where(group == block, counts[plane, block], count)
        live = slot < count
        row_cell = row_here[source].astype(jnp.float32)
        z_cell = z_here[source]
        for offset in range(4):
            weight_x = kernel_weight(float(offset - 1) - fractions_here[0, source])
            for part in range(3):
                rows[part * 4 + offset] = jnp.where(live, strength_here[part, source] * weight_x, 0.0)
            rows[12 + offset] = kernel_weight(float(offset - 1) - fractions_here[1, source])
            rows[16 + offset] = row_cell + float(offset)
            rows[20 + offset] = kernel_weight(float(offset - 1) - fractions_here[2, source])
            rows[24 + offset] = jnp.bitwise_and(z_cell + offset, NZ - 1).astype(jnp.float32)

        used = [(part, offset) for part in range(3) for offset in offsets]

        def spread(block, first):
            here = slice(first, first + width)

            def row(index):
                return rows[index, block : block + 1, here]

            weight_y = jnp.zeros((ext, width), jnp.float32)
            for offset in range(4):
                weight_y = jnp.where(j_iota == row(16 + offset), row(12 + offset), weight_y)
            coefs = jnp.concatenate([row(p * 4 + o) * weight_y for p, o in used], axis=0)
            coefs = coefs.astype(jnp.bfloat16)
            z_weight = [
                jnp.broadcast_to(row(20 + offset), (z_rows, width)).astype(jnp.bfloat16)
                for offset in range(4)
            ]
            z_place = [
                jnp.broadcast_to(row(24 + offset), (z_rows, width)).astype(jnp.bfloat16)
                for offset in range(4)
            ]
            tiles = []
            for z_tile in z_tiles:
                tile = jnp.zeros((z_rows, width), jnp.bfloat16)
                for offset in range(4):
                    tile = jnp.where(z_tile == z_place[offset], z_weight[offset], tile)
                tiles.append(tile)
            weight_z = jnp.concatenate(tiles, axis=0)
            result = lax.dot_general(
                coefs, weight_z, (((1,), (1,)), ((), ())), preferred_element_type=jnp.float32
            )
            low = block * BLOCK_ROWS
            for index, (part, offset) in enumerate(used):
                grid[part, plane + offset - begin, low : low + ext, :] += result[
                    index * ext : (index + 1) * ext
                ]

        for block in range(blocks):
            spread(block, 0)
        for first in range(width, slots, width):
            for block in range(blocks):
                pl.when(counts[plane, block] > first)(functools.partial(spread, block, first))
        return 0

    top = end + 3 if last else end
    inner_begin, inner_end = begin, top - 3
    for plane in range(first_source, begin):
        offsets = [o for o in range(4) if begin <= plane + o]
        one_plane(offsets, plane - first_source, 0)
    lax.fori_loop(
        inner_begin - first_source,
        inner_end - first_source,
        functools.partial(one_plane, list(range(4))),
        0,
    )
    for plane in range(inner_end, end):
        offsets = [o for o in range(4) if plane + o < top]
        one_plane(offsets, plane - first_source, 0)

    def side(plane, _):
        ghost_y[:, plane] = grid[:, plane, rows_local : rows_local + 3, :]
        return 0

    lax.fori_loop(0, end - begin, side, 0)
    if last:
        for part in range(3):
            for offset in range(3):
                plane = end - begin + offset
                ghost_x[part, offset] = grid[part, plane, :rows_local, :]
                ghost_xy[part, offset] = grid[part, plane, rows_local : rows_local + 3, :]


def deposit(particles, begin, end):
    planes, blocks, slots = particles[1].shape
    sources = end - max(begin - 3, 0)
    rows_local = blocks * BLOCK_ROWS
    whole = pl.BlockSpec(memory_space=pltpu.VMEM)
    last = end == planes
    shapes = [(3, end - begin + (3 if last else 0), rows_local + 8, NZ), (3, end - begin, 3, NZ)]
    if last:
        shapes += [(3, 3, rows_local, NZ), (3, 3, 3, NZ)]
    return pl.pallas_call(
        functools.partial(deposit_kernel, begin, end),
        out_shape=[jax.ShapeDtypeStruct(shape, jnp.float32) for shape in shapes],
        in_specs=[pl.BlockSpec(memory_space=pltpu.SMEM)]
        + [pl.BlockSpec(memory_space=pltpu.HBM)] * 4,
        out_specs=[whole] * len(shapes),
        scratch_shapes=[
            pltpu.VMEM((28, blocks, slots), jnp.float32),
            pltpu.VMEM((sources, blocks, slots), jnp.int32),
            pltpu.VMEM((sources, blocks, slots), jnp.int32),
            pltpu.VMEM((3, sources, blocks, slots), jnp.float32),
            pltpu.VMEM((3, sources, blocks, slots), jnp.float32),
            pltpu.SemaphoreType.DMA((4,)),
        ],
        compiler_params=vmem(),
        cost_estimate=cost(10 * sources * blocks * 288 * slots * NZ, 12 * MIB),
        name="deposit",
    )(*particles)


def next_over(block, axes):
    counts = [lax.axis_size(axis) for axis in AXES]
    route = []
    for slab in range(counts[0]):
        for pen in range(counts[1]):
            to_slab = (slab + 1) % counts[0] if "slab" in axes else slab
            to_pen = (pen + 1) % counts[1] if "pen" in axes else pen
            route.append((slab * counts[1] + pen, to_slab * counts[1] + to_pen))
    return lax.ppermute(block, AXES, route)


def shifted(block, axis, distance):
    count = lax.axis_size(axis)
    return lax.ppermute(block, axis, [(i, (i + distance) % count) for i in range(count)])


def z_forward_body(with_x, grid, ghost_y, *refs):
    vorticity, send = refs[-2:]
    table = refs[-3]
    rows_local = vorticity.shape[2]
    vorticity[0] = grid[0, :, :rows_local, :]
    vorticity[0, :, 0:3, :] += ghost_y[0]
    if with_x:
        ghost_x, ghost_xy = refs[:2]

        @pl.when(pl.program_id(1) == 0)
        def _():
            vorticity[0, 0:3] += ghost_x[0]
            vorticity[0, 0:3, 0:3, :] += ghost_xy[0]

    spectrum = times_right(vorticity[0].reshape(STEP * rows_local, NZ), table[...])
    lines = send.reshape(HALF * STEP, 2 * rows_local)
    for plane in range(STEP):
        here = spectrum[plane * rows_local : (plane + 1) * rows_local]
        stacked = jnp.concatenate([here[:, :HALF], here[:, HALF:]], axis=0)
        lines[pl.ds(plane, HALF, stride=STEP), :] = stacked.T


def z_forward(parts, cell_range, deposited, ghosts_x, vorticity, send, shape):
    devices, depth, planes, width = shape
    begin, end = cell_range
    grid, ghost_y = deposited
    rows_local = width // 2
    count = len(parts)
    part = parts[0]
    table = right_table(z_forward_table())
    here = (end - begin) // STEP
    at = begin // STEP
    joined = send is not None
    send_at = at if joined else 0
    send_planes = planes if joined else end - begin
    specs = [
        pl.BlockSpec((1, STEP, rows_local + 8, NZ), lambda c, i: (part + c, i, 0, 0)),
        pl.BlockSpec((1, STEP, 3, NZ), lambda c, i: (part + c, i, 0, 0)),
    ]
    operands = [grid, ghost_y]
    if ghosts_x is not None:
        operands += list(ghosts_x)
        specs += [
            pl.BlockSpec((1, 3, rows_local, NZ), lambda c, i: (part + c, 0, 0, 0)),
            pl.BlockSpec((1, 3, 3, NZ), lambda c, i: (part + c, 0, 0, 0)),
        ]
    operands.append(table)
    specs.append(pl.BlockSpec(table.shape, lambda c, i: (0, 0)))
    aliases = {}
    for index, output in enumerate((vorticity, send)):
        if output is not None and output is not NEW:
            aliases[len(operands)] = index
            specs.append(pl.BlockSpec(memory_space=pl.ANY))
            operands.append(output)
    used = 5 if ghosts_x is not None else 3

    def kernel(*refs):
        z_forward_body(ghosts_x is not None, *refs[:used], *refs[-2:])

    return pl.pallas_call(
        kernel,
        grid=(count, here),
        in_specs=specs,
        out_specs=(
            pl.BlockSpec((1, STEP, rows_local, NZ), lambda c, i: (part + c, at + i, 0, 0)),
            pl.BlockSpec(
                (devices, None, depth, STEP, width), lambda c, i: (0, c, 0, send_at + i, 0)
            ),
        ),
        out_shape=(
            jax.ShapeDtypeStruct((3, planes, rows_local, NZ), jnp.float32),
            jax.ShapeDtypeStruct((devices, count, depth, send_planes, width), jnp.float32),
        ),
        input_output_aliases=aliases,
        compiler_params=vmem(),
        cost_estimate=cost(
            6 * count * here * STEP * rows_local * NZ * NZ,
            3 * count * here * STEP * rows_local * NZ * 4,
        ),
        name="z_forward",
    )(*operands)


def z_inverse_kernel(received, table, field, low_x, high_x, low_y, high_y):
    rows_local = field.shape[1]
    lines = received.reshape(HALF * STEP, 2 * rows_local)
    pieces = []
    for plane in range(STEP):
        turned = lines[pl.ds(plane, HALF, stride=STEP), :].T
        pieces.append(jnp.concatenate([turned[:rows_local], turned[rows_local:]], axis=1))
    values = times_right(jnp.concatenate(pieces, axis=0), table[...])
    field[...] = values.reshape(STEP, rows_local, NZ)
    low_y[...] = field[:, 0:2, :]
    high_y[...] = field[:, rows_local - 2 : rows_local, :]

    @pl.when(pl.program_id(0) == 0)
    def _():
        low_x[...] = field[0:2]

    @pl.when(pl.program_id(0) == pl.num_programs(0) - 1)
    def _():
        high_x[...] = field[STEP - 2 : STEP]


def z_inverse(received):
    devices, depth, planes, width = received.shape
    rows_local = width // 2
    table = right_table(z_inverse_table())
    layer = pl.BlockSpec((2, rows_local, NZ), lambda i: (0, 0, 0))
    edge = pl.BlockSpec((STEP, 2, NZ), lambda i: (i, 0, 0))
    return pl.pallas_call(
        z_inverse_kernel,
        grid=(planes // STEP,),
        in_specs=[
            pl.BlockSpec((devices, depth, STEP, width), lambda i: (0, 0, i, 0)),
            pl.BlockSpec(table.shape, lambda i: (0, 0)),
        ],
        out_specs=(
            pl.BlockSpec((STEP, rows_local, NZ), lambda i: (i, 0, 0)),
            layer,
            layer,
            edge,
            edge,
        ),
        out_shape=(
            jax.ShapeDtypeStruct((planes, rows_local, NZ), jnp.float32),
            jax.ShapeDtypeStruct((2, rows_local, NZ), jnp.float32),
            jax.ShapeDtypeStruct((2, rows_local, NZ), jnp.float32),
            jax.ShapeDtypeStruct((planes, 2, NZ), jnp.float32),
            jax.ShapeDtypeStruct((planes, 2, NZ), jnp.float32),
        ),
        compiler_params=vmem(),
        cost_estimate=cost(
            6 * planes * rows_local * NZ * NZ, 2 * planes * rows_local * NZ * 4
        ),
        name="z_inverse",
    )(received, table)


def plane_forward_kernel(start, *refs):
    y_table, x_table_ref, spectrum = refs[-3:]
    received = refs[:-3]
    step = pl.program_id(1)
    depth = pl.num_programs(1) - 1
    has_first = start[0] == 0

    @pl.when(jnp.logical_or(step < depth, has_first))
    def _():
        slabs, pens, _, width = received[0].shape
        pieces = []
        for pen in range(pens):
            piece = jnp.concatenate([cells[:, pen] for cells in received], axis=1)
            pieces.append(piece.reshape(slabs * piece.shape[1], width))
        lane = lax.broadcasted_iota(jnp.int32, (1, width), 1)
        real_side = lane < width // 2
        keep_real = jnp.logical_or(real_side, jnp.logical_not(jnp.logical_and(has_first, step == 0)))
        keep_imaginary = jnp.logical_or(jnp.logical_not(real_side), step < depth)
        keep = jnp.logical_and(keep_real, keep_imaginary).astype(jnp.float32)
        lines = jnp.concatenate([piece * keep for piece in pieces], axis=1)
        along_y = times_right(lines, y_table[...])
        rows_y = along_y.shape[1] // 2
        stacked = jnp.concatenate([along_y[:, :rows_y], along_y[:, rows_y:]], axis=0)
        spectrum[...] = times_left(x_table_ref[...], stacked)


def plane_forward(start, received):
    slabs, pens, count, depth, _, width = received[0].shape
    size_x = slabs * sum(cells.shape[4] for cells in received)
    size_y = pens * (width // 2)
    y_table = right_table(y_forward_table(size_y, pens))
    x_matrix = left_table(x_table(size_x, -1.0))
    return pl.pallas_call(
        plane_forward_kernel,
        grid=(count, depth + 1),
        in_specs=[pl.BlockSpec(memory_space=pltpu.SMEM)]
        + [
            pl.BlockSpec(
                (slabs, pens, None, None, cells.shape[4], width),
                lambda c, j: (0, 0, c, jnp.where(j < depth, j, 0), 0, 0),
            )
            for cells in received
        ]
        + [
            pl.BlockSpec(y_table.shape, lambda c, j: (0, 0)),
            pl.BlockSpec(x_matrix.shape, lambda c, j: (0, 0)),
        ],
        out_specs=pl.BlockSpec((None, None, 2 * size_x, size_y), lambda c, j: (c, j, 0, 0)),
        out_shape=jax.ShapeDtypeStruct((count, depth + 1, 2 * size_x, size_y), jnp.float32),
        compiler_params=vmem(),
        cost_estimate=cost(
            24 * count * depth * size_x * size_y * (size_x + size_y),
            4 * count * depth * size_x * size_y * 4,
        ),
        name="plane_forward",
    )(start, *received, y_table, x_matrix)


def wave_pair(shape, dim, length):
    index = lax.broadcasted_iota(jnp.int32, shape, dim)
    signed_index = jnp.where(index < length // 2, index, index - length)
    full_wave = (2.0 * math.pi / length) * signed_index.astype(jnp.float32)
    return full_wave, jnp.where(index == length // 2, 0.0, full_wave)


def plane_inverse_kernel(parts, needs, start, *refs):
    spectra = dict(zip(needs, refs[: len(needs)]))
    extras = dict(zip(needs, refs[len(needs) : 2 * len(needs)]))
    y_table, x_table_ref = refs[2 * len(needs) : 2 * len(needs) + 2]
    backs, turned = refs[2 * len(needs) + 2 : -1], refs[-1]
    step = pl.program_id(0)
    size_x, size_y = turned.shape[1] // 2, turned.shape[2]
    full_x, curl_x = wave_pair((size_x, 1), 0, size_x)
    full_y, curl_y = wave_pair((1, size_y), 1, size_y)

    def curl(part, source, full_z, curl_z):
        curls = (curl_x, curl_y, curl_z)
        wave_left, wave_right = curls[(part + 1) % 3], curls[(part + 2) % 3]
        left, right = source[(part + 1) % 3], source[(part + 2) % 3]
        wave_squared = full_x * full_x + full_y * full_y + full_z * full_z
        present = wave_squared > 0.0
        scaling = jnp.where(present, 1.0 / jnp.where(present, wave_squared, 1.0), 0.0)
        scaling = scaling * (1.0 / float(size_x * size_y * NZ))
        real_part = wave_left * right[:size_x] - wave_right * left[:size_x]
        imaginary = wave_left * right[size_x:] - wave_right * left[size_x:]
        return -imaginary * scaling, real_part * scaling

    index_z = (start[0] + step).astype(jnp.float32)
    wave_z = (2.0 * math.pi / NZ) * index_z
    for at, part in enumerate(parts):
        real_part, imaginary = curl(part, spectra, wave_z, wave_z)
        turned[at, :size_x] = real_part
        turned[at, size_x:] = imaginary

    @pl.when(jnp.logical_and(start[0] == 0, step == 0))
    def _():
        for at, part in enumerate(parts):
            extra_real, extra_imaginary = curl(part, extras, -math.pi, 0.0)
            turned[at, :size_x] += extra_real
            turned[at, size_x:] += extra_imaginary

    slabs, pens, planes, width = backs[0].shape
    for at, back in enumerate(backs):
        along_x = times_left(x_table_ref[...], turned[at])
        lines = jnp.concatenate([along_x[:size_x], along_x[size_x:]], axis=1)
        result = times_right(lines, y_table[...])
        for pen in range(pens):
            piece = result[:, pen * width : (pen + 1) * width]
            back[:, pen] = piece.reshape(slabs, planes, width)


def plane_inverse(parts, start, spectra, shape):
    slabs, pens, depth, planes, width = shape
    count = len(parts)
    size_x = slabs * planes
    size_y = pens * (width // 2)
    y_table = right_table(y_inverse_table(size_y, pens))
    x_matrix = left_table(x_table(size_x, 1.0))
    needs = [c for c in range(3) if any(c != part for part in parts)]

    def at(index, extra):
        return pl.BlockSpec(
            (None, None, 2 * size_x, size_y),
            lambda j: (index, depth if extra else j, 0, 0),
        )

    return pl.pallas_call(
        functools.partial(plane_inverse_kernel, parts, needs),
        grid=(depth,),
        in_specs=[pl.BlockSpec(memory_space=pltpu.SMEM)]
        + [at(spectra[c][1], False) for c in needs]
        + [at(spectra[c][1], True) for c in needs]
        + [
            pl.BlockSpec(y_table.shape, lambda j: (0, 0)),
            pl.BlockSpec(x_matrix.shape, lambda j: (0, 0)),
        ],
        out_specs=[
            pl.BlockSpec((slabs, pens, None, planes, width), lambda j: (0, 0, j, 0, 0))
        ]
        * count,
        out_shape=[jax.ShapeDtypeStruct(shape, jnp.float32)] * count,
        scratch_shapes=[pltpu.VMEM((count, 2 * size_x, size_y), jnp.float32)],
        compiler_params=vmem(),
        cost_estimate=cost(
            24 * count * depth * size_x * size_y * (size_x + size_y),
            6 * count * depth * size_x * size_y * 4,
        ),
        name="plane_inverse",
    )(start, *([spectra[c][0] for c in needs] * 2), y_table, x_matrix)


def z_difference_table():
    table = np.zeros((NZ, NZ), np.float32)
    for cell in range(NZ):
        for shift, weight in ((1, 8.0), (-1, -8.0), (2, -1.0), (-2, 1.0)):
            table[(cell + shift) % NZ, cell] += weight
    table = table.astype(jnp.bfloat16)
    return jnp.asarray(np.concatenate([table, table], axis=0))


def stretch_kernel(vorticity, field, before, after, low_x, high_x, low_y, high_y, table, *refs):
    velocity, stretching, padded = refs[-3:]
    step = pl.program_id(0)
    rows_local = field.shape[1]
    first = step == 0
    last = step == pl.num_programs(0) - 1
    own = slice(8, 8 + rows_local)
    for plane in range(STEP):
        padded[plane, own, :] = field[plane]
        padded[plane, 6:8, :] = low_y[plane]
        padded[plane, 8 + rows_local : 10 + rows_local, :] = high_y[plane]
    high, low = split_values(field[...].reshape(STEP * rows_local, NZ))
    along_z = jnp.dot(
        jnp.concatenate([high, low], axis=1), table[...], preferred_element_type=jnp.float32
    )

    def difference(ahead, behind, ahead_2, behind_2):
        return 8.0 * (ahead - behind) - (ahead_2 - behind_2)

    def along(plane):
        if plane < 0:
            return jnp.where(first, low_x[plane + 2], before[plane + 2])
        if plane >= STEP:
            return jnp.where(last, high_x[plane - STEP], after[plane - STEP])
        return field[plane]

    for plane in range(STEP):
        velocity[0, plane] = field[plane]
        along_x = difference(*(along(plane + shift) for shift in (1, -1, 2, -2)))
        along_y = difference(
            *(padded[plane, 8 + shift : 8 + shift + rows_local, :] for shift in (1, -1, 2, -2))
        )
        total = vorticity[0, plane] * along_x + vorticity[1, plane] * along_y
        total = total + vorticity[2, plane] * along_z[plane * rows_local : (plane + 1) * rows_local]
        stretching[0, plane] = total * (1.0 / 12.0)


def stretch(part, vorticity, field, halos, outputs):
    planes, rows_local, _ = field.shape
    pairs = STEP // 2
    table = z_difference_table()
    layer = pl.BlockSpec((2, rows_local, NZ), lambda i: (0, 0, 0))
    edge = pl.BlockSpec((STEP, 2, NZ), lambda i: (i, 0, 0))
    block = pl.BlockSpec((1, STEP, rows_local, NZ), lambda i: (part, i, 0, 0))
    specs = [
        pl.BlockSpec((3, STEP, rows_local, NZ), lambda i: (0, i, 0, 0)),
        pl.BlockSpec((STEP, rows_local, NZ), lambda i: (i, 0, 0)),
        pl.BlockSpec((2, rows_local, NZ), lambda i: (jnp.maximum(i * pairs - 1, 0), 0, 0)),
        pl.BlockSpec(
            (2, rows_local, NZ), lambda i: (jnp.minimum((i + 1) * pairs, planes // 2 - 1), 0, 0)
        ),
        layer,
        layer,
        edge,
        edge,
        pl.BlockSpec(table.shape, lambda i: (0, 0)),
    ]
    operands = [vorticity, field, field, field, *halos, table]
    aliases = {}
    if outputs is not None:
        aliases = {len(operands): 0, len(operands) + 1: 1}
        specs += [pl.BlockSpec(memory_space=pl.ANY)] * 2
        operands += list(outputs)
    shape = jax.ShapeDtypeStruct((3, planes, rows_local, NZ), jnp.float32)
    return pl.pallas_call(
        stretch_kernel,
        grid=(planes // STEP,),
        in_specs=specs,
        out_specs=(block, block),
        out_shape=(shape, shape),
        input_output_aliases=aliases,
        scratch_shapes=[pltpu.VMEM((STEP, rows_local + 16, NZ), jnp.float32)],
        compiler_params=vmem(),
        cost_estimate=cost(600 * planes * rows_local * NZ, 7 * planes * rows_local * NZ * 4),
        name="stretch",
    )(*operands)


def per_device(counts, row_base, z_base, fractions, strength):
    slabs, pens = lax.axis_size("slab"), lax.axis_size("pen")
    devices = slabs * pens
    depth = HALF // devices
    planes, blocks, _ = row_base.shape
    rows_local = blocks * BLOCK_ROWS
    width = 2 * rows_local
    place = lax.axis_index("slab") * pens + lax.axis_index("pen")
    start = (place * depth).astype(jnp.int32).reshape(1)
    shape = (devices, depth, planes, width)

    def exchange(blocks_out, after=None):
        if after is not None:
            blocks_out, _ = lax.optimization_barrier((blocks_out, after))
        return lax.all_to_all(blocks_out, AXES, 0, 0, tiled=True)

    def unfold(received):
        return received.reshape((slabs, pens) + received.shape[1:])

    cut = planes - STEP
    particles = (counts, row_base, z_base, fractions, strength)
    grid, ghost_y, ghost_x, ghost_xy = deposit(particles, cut, planes)
    tail = (grid, next_over(ghost_y, ("pen",)))
    ghosts_x = (next_over(ghost_x, ("slab",)), next_over(ghost_xy, ("slab", "pen")))
    everything = (cut, planes)
    if cut == 0:
        vorticity, send = z_forward((1, 2), everything, tail, ghosts_x, None, None, shape)
        received = [exchange(send)]
        vorticity, send = z_forward((0,), everything, tail, ghosts_x, vorticity, None, shape)
    else:
        vorticity, send = z_forward((1, 2), everything, tail, None, None, None, shape)
        held, _ = lax.optimization_barrier((particles, send))
        grid, ghost_y = deposit(held, 0, cut)
        head = (grid, next_over(ghost_y, ("pen",)))
        received = [exchange(send)]
        vorticity, send = z_forward((1, 2), (0, cut), head, ghosts_x, vorticity, None, shape)
        received = [exchange(send, received[0])] + received
        vorticity, send = z_forward((0,), (0, cut), head, ghosts_x, vorticity, NEW, shape)
        vorticity, send = z_forward((0,), everything, tail, None, vorticity, send, shape)
    pair = plane_forward(start, [unfold(cells) for cells in received])
    single = plane_forward(start, [unfold(exchange(send, received[0]))])
    spectra = {1: (pair, 0), 2: (pair, 1), 0: (single, 0)}

    shape = (slabs, pens, depth, planes, width)
    backs = plane_inverse((0,), start, spectra, shape) + plane_inverse((1, 2), start, spectra, shape)
    outputs = received = None
    for part, back in enumerate(backs):
        received = exchange(back.reshape(devices, depth, planes, width), received)
        field, low_x, high_x, low_y, high_y = z_inverse(received)
        halos = (
            shifted(high_x, "slab", 1),
            shifted(low_x, "slab", -1),
            shifted(high_y, "pen", 1),
            shifted(low_y, "pen", -1),
        )
        outputs = stretch(part, vorticity, field, halos, outputs)
    return (vorticity, outputs[0], outputs[1])


def solution(mesh):
    in_specs = (
        P("slab", "pen"),
        P("slab", "pen", None),
        P("slab", "pen", None),
        P(None, "slab", "pen", None),
        P(None, "slab", "pen", None),
    )
    out_specs = (
        P(None, "slab", "pen", None),
        P(None, "slab", "pen", None),
        P(None, "slab", "pen", None),
    )
    return jax.shard_map(
        per_device, mesh=mesh, in_specs=in_specs, out_specs=out_specs, check_vma=False
    )
```

```python
import functools
import math

import jax
import jax.numpy as jnp
import numpy as np
from jax import lax
from jax.experimental import pallas as pl
from jax.experimental.pallas import tpu as pltpu
from jax.sharding import PartitionSpec as P

NZ = 256
BLOCK_ROWS = 16
HALF = NZ // 2
STEP = 8
SLOTS_AT_ONCE = 256
MIB = 1024 * 1024
NEW = object()
AXES = ("slab", "pen")


def kernel_weight(distance):
    magnitude = jnp.abs(distance)
    inner_part = 1.0 - 2.5 * magnitude * magnitude + 1.5 * magnitude * magnitude * magnitude
    outer_part = 0.5 * (2.0 - magnitude) * (2.0 - magnitude) * (1.0 - magnitude)
    return jnp.where(magnitude < 1.0, inner_part, jnp.where(magnitude < 2.0, outer_part, 0.0))


def vmem(limit=48, **extra):
    return pltpu.CompilerParams(vmem_limit_bytes=limit * MIB, **extra)


def cost(flops, moved):
    return pl.CostEstimate(flops=int(flops), bytes_accessed=int(moved), transcendentals=0)


def two_parts(table):
    table = np.asarray(table, np.float32)
    high = table.astype(jnp.bfloat16)
    low = (table - high.astype(np.float32)).astype(jnp.bfloat16)
    return high, low


def right_table(table):
    high, low = two_parts(table)
    return jnp.asarray(np.concatenate([high, high, low], axis=0))


def left_table(table):
    high, low = two_parts(table)
    return jnp.asarray(np.concatenate([high, high, low], axis=1))


def waves(length):
    index = np.arange(length)
    angle = 2.0 * np.pi / length * (index[:, None] * index[None, :] % length)
    return np.cos(angle), np.sin(angle)


def z_forward_table():
    cosine, sine = waves(NZ)
    real_part, imaginary = cosine[:, :HALF].copy(), -sine[:, :HALF]
    imaginary[:, 0] = cosine[:, HALF]
    return np.concatenate([real_part, imaginary], axis=1)


def z_inverse_table():
    cosine, sine = waves(NZ)
    real_part, imaginary = 2.0 * cosine[:HALF], -2.0 * sine[:HALF]
    real_part[0] = 1.0
    imaginary[0] = cosine[HALF]
    return np.concatenate([real_part, imaginary], axis=0)


def y_forward_table(length, parts):
    cosine, sine = waves(length)
    width = length // parts
    rows = []
    for part in range(parts):
        here = slice(part * width, (part + 1) * width)
        rows.append(np.concatenate([cosine[here], -sine[here]], axis=1))
        rows.append(np.concatenate([sine[here], cosine[here]], axis=1))
    return np.concatenate(rows, axis=0)


def y_inverse_table(length, parts):
    cosine, sine = waves(length)
    width = length // parts
    columns = []
    for part in range(parts):
        here = slice(part * width, (part + 1) * width)
        columns.append(np.concatenate([cosine[:, here], -sine[:, here]], axis=0))
        columns.append(np.concatenate([sine[:, here], cosine[:, here]], axis=0))
    return np.concatenate(columns, axis=1)


def x_table(length, sign):
    cosine, sine = waves(length)
    return np.concatenate(
        [
            np.concatenate([cosine, -sign * sine], axis=1),
            np.concatenate([sign * sine, cosine], axis=1),
        ],
        axis=0,
    )


def split_values(values):
    high = values.astype(jnp.bfloat16)
    low = (values - high.astype(jnp.float32)).astype(jnp.bfloat16)
    return high, low


def times_right(values, table):
    high, low = split_values(values)
    return jnp.dot(
        jnp.concatenate([high, low, high], axis=1), table, preferred_element_type=jnp.float32
    )


def times_left(table, values):
    high, low = split_values(values)
    return jnp.dot(
        table, jnp.concatenate([high, low, high], axis=0), preferred_element_type=jnp.float32
    )


def deposit_kernel(begin, end, counts, row_base, z_base, fractions, strength, *refs):
    planes, blocks, slots = row_base.shape
    first_source = max(begin - 3, 0)
    last = end == planes
    width = min(SLOTS_AT_ONCE, slots)
    rows_local = blocks * BLOCK_ROWS
    ext = BLOCK_ROWS + 8
    if last:
        grid, ghost_y, ghost_x, ghost_xy = refs[:4]
    else:
        grid, ghost_y = refs[:2]
    rows, row_here, z_here, fractions_here, strength_here, arrived = refs[-6:]
    taken = slice(first_source, end)
    copies = [
        pltpu.make_async_copy(row_base.at[taken], row_here, arrived.at[0]),
        pltpu.make_async_copy(z_base.at[taken], z_here, arrived.at[1]),
        pltpu.make_async_copy(fractions.at[:, taken], fractions_here, arrived.at[2]),
        pltpu.make_async_copy(strength.at[:, taken], strength_here, arrived.at[3]),
    ]
    for copy in copies:
        copy.start()

    def clear(plane, _):
        grid[:, plane] = jnp.zeros((3,) + grid.shape[2:], jnp.float32)
        return 0

    lax.fori_loop(0, grid.shape[1], clear, 0)
    z_rows = 16
    z_iota = lax.broadcasted_iota(jnp.int32, (z_rows, width), 0)
    j_iota = lax.broadcasted_iota(jnp.int32, (ext, width), 0).astype(jnp.float32)
    z_tiles = [
        (z_iota + z_rows * t).astype(jnp.float32).astype(jnp.bfloat16) for t in range(NZ // z_rows)
    ]
    for copy in copies:
        copy.wait()

    def one_plane(offsets, source, _):
        plane = source + first_source
        slot = lax.broadcasted_iota(jnp.int32, (blocks, slots), 1)
        group = lax.broadcasted_iota(jnp.int32, (blocks, slots), 0)
        count = jnp.zeros((blocks, slots), jnp.int32)
        for block in range(blocks):
            count = jnp.where(group == block, counts[plane, block], count)
        live = slot < count
        row_cell = row_here[source].astype(jnp.float32)
        z_cell = z_here[source]
        for offset in range(4):
            weight_x = kernel_weight(float(offset - 1) - fractions_here[0, source])
            for part in range(3):
                rows[part * 4 + offset] = jnp.where(live, strength_here[part, source] * weight_x, 0.0)
            rows[12 + offset] = kernel_weight(float(offset - 1) - fractions_here[1, source])
            rows[16 + offset] = row_cell + float(offset)
            rows[20 + offset] = kernel_weight(float(offset - 1) - fractions_here[2, source])
            rows[24 + offset] = jnp.bitwise_and(z_cell + offset, NZ - 1).astype(jnp.float32)

        used = [(part, offset) for part in range(3) for offset in offsets]

        def spread(block, first):
            here = slice(first, first + width)

            def row(index):
                return rows[index, block : block + 1, here]

            weight_y = jnp.zeros((ext, width), jnp.float32)
            for offset in range(4):
                weight_y = jnp.where(j_iota == row(16 + offset), row(12 + offset), weight_y)
            coefs = jnp.concatenate([row(p * 4 + o) * weight_y for p, o in used], axis=0)
            coefs = coefs.astype(jnp.bfloat16)
            z_weight = [
                jnp.broadcast_to(row(20 + offset), (z_rows, width)).astype(jnp.bfloat16)
                for offset in range(4)
            ]
            z_place = [
                jnp.broadcast_to(row(24 + offset), (z_rows, width)).astype(jnp.bfloat16)
                for offset in range(4)
            ]
            tiles = []
            for z_tile in z_tiles:
                tile = jnp.zeros((z_rows, width), jnp.bfloat16)
                for offset in range(4):
                    tile = jnp.where(z_tile == z_place[offset], z_weight[offset], tile)
                tiles.append(tile)
            weight_z = jnp.concatenate(tiles, axis=0)
            result = lax.dot_general(
                coefs, weight_z, (((1,), (1,)), ((), ())), preferred_element_type=jnp.float32
            )
            low = block * BLOCK_ROWS
            for index, (part, offset) in enumerate(used):
                grid[part, plane + offset - begin, low : low + ext, :] += result[
                    index * ext : (index + 1) * ext
                ]

        for block in range(blocks):
            spread(block, 0)
        for first in range(width, slots, width):
            for block in range(blocks):
                pl.when(counts[plane, block] > first)(functools.partial(spread, block, first))
        return 0

    top = end + 3 if last else end
    inner_begin, inner_end = begin, top - 3
    for plane in range(first_source, begin):
        offsets = [o for o in range(4) if begin <= plane + o]
        one_plane(offsets, plane - first_source, 0)
    lax.fori_loop(
        inner_begin - first_source,
        inner_end - first_source,
        functools.partial(one_plane, list(range(4))),
        0,
    )
    for plane in range(inner_end, end):
        offsets = [o for o in range(4) if plane + o < top]
        one_plane(offsets, plane - first_source, 0)

    def side(plane, _):
        ghost_y[:, plane] = grid[:, plane, rows_local : rows_local + 3, :]
        return 0

    lax.fori_loop(0, end - begin, side, 0)
    if last:
        for part in range(3):
            for offset in range(3):
                plane = end - begin + offset
                ghost_x[part, offset] = grid[part, plane, :rows_local, :]
                ghost_xy[part, offset] = grid[part, plane, rows_local : rows_local + 3, :]


def deposit(particles, begin, end):
    planes, blocks, slots = particles[1].shape
    sources = end - max(begin - 3, 0)
    rows_local = blocks * BLOCK_ROWS
    whole = pl.BlockSpec(memory_space=pltpu.VMEM)
    last = end == planes
    shapes = [(3, end - begin + (3 if last else 0), rows_local + 8, NZ), (3, end - begin, 3, NZ)]
    if last:
        shapes += [(3, 3, rows_local, NZ), (3, 3, 3, NZ)]
    return pl.pallas_call(
        functools.partial(deposit_kernel, begin, end),
        out_shape=[jax.ShapeDtypeStruct(shape, jnp.float32) for shape in shapes],
        in_specs=[pl.BlockSpec(memory_space=pltpu.SMEM)]
        + [pl.BlockSpec(memory_space=pltpu.HBM)] * 4,
        out_specs=[whole] * len(shapes),
        scratch_shapes=[
            pltpu.VMEM((28, blocks, slots), jnp.float32),
            pltpu.VMEM((sources, blocks, slots), jnp.int32),
            pltpu.VMEM((sources, blocks, slots), jnp.int32),
            pltpu.VMEM((3, sources, blocks, slots), jnp.float32),
            pltpu.VMEM((3, sources, blocks, slots), jnp.float32),
            pltpu.SemaphoreType.DMA((4,)),
        ],
        compiler_params=vmem(),
        cost_estimate=cost(10 * sources * blocks * 288 * slots * NZ, 12 * MIB),
        name="deposit",
    )(*particles)


def next_over(block, axes):
    counts = [lax.axis_size(axis) for axis in AXES]
    route = []
    for slab in range(counts[0]):
        for pen in range(counts[1]):
            to_slab = (slab + 1) % counts[0] if "slab" in axes else slab
            to_pen = (pen + 1) % counts[1] if "pen" in axes else pen
            route.append((slab * counts[1] + pen, to_slab * counts[1] + to_pen))
    return lax.ppermute(block, AXES, route)


def shifted(block, axis, distance):
    count = lax.axis_size(axis)
    return lax.ppermute(block, axis, [(i, (i + distance) % count) for i in range(count)])


def z_forward_body(with_x, grid, ghost_y, *refs):
    vorticity, send = refs[-2:]
    table = refs[-3]
    rows_local = vorticity.shape[2]
    vorticity[0] = grid[0, :, :rows_local, :]
    vorticity[0, :, 0:3, :] += ghost_y[0]
    if with_x:
        ghost_x, ghost_xy = refs[:2]

        @pl.when(pl.program_id(1) == 0)
        def _():
            vorticity[0, 0:3] += ghost_x[0]
            vorticity[0, 0:3, 0:3, :] += ghost_xy[0]

    spectrum = times_right(vorticity[0].reshape(STEP * rows_local, NZ), table[...])
    lines = send.reshape(HALF * STEP, 2 * rows_local)
    for plane in range(STEP):
        here = spectrum[plane * rows_local : (plane + 1) * rows_local]
        stacked = jnp.concatenate([here[:, :HALF], here[:, HALF:]], axis=0)
        lines[pl.ds(plane, HALF, stride=STEP), :] = stacked.T


def z_forward(parts, cell_range, deposited, ghosts_x, vorticity, send, shape):
    devices, depth, planes, width = shape
    begin, end = cell_range
    grid, ghost_y = deposited
    rows_local = width // 2
    count = len(parts)
    part = parts[0]
    table = right_table(z_forward_table())
    here = (end - begin) // STEP
    at = begin // STEP
    joined = send is not None
    send_at = at if joined else 0
    send_planes = planes if joined else end - begin
    specs = [
        pl.BlockSpec((1, STEP, rows_local + 8, NZ), lambda c, i: (part + c, i, 0, 0)),
        pl.BlockSpec((1, STEP, 3, NZ), lambda c, i: (part + c, i, 0, 0)),
    ]
    operands = [grid, ghost_y]
    if ghosts_x is not None:
        operands += list(ghosts_x)
        specs += [
            pl.BlockSpec((1, 3, rows_local, NZ), lambda c, i: (part + c, 0, 0, 0)),
            pl.BlockSpec((1, 3, 3, NZ), lambda c, i: (part + c, 0, 0, 0)),
        ]
    operands.append(table)
    specs.append(pl.BlockSpec(table.shape, lambda c, i: (0, 0)))
    aliases = {}
    for index, output in enumerate((vorticity, send)):
        if output is not None and output is not NEW:
            aliases[len(operands)] = index
            specs.append(pl.BlockSpec(memory_space=pl.ANY))
            operands.append(output)
    used = 5 if ghosts_x is not None else 3

    def kernel(*refs):
        z_forward_body(ghosts_x is not None, *refs[:used], *refs[-2:])

    return pl.pallas_call(
        kernel,
        grid=(count, here),
        in_specs=specs,
        out_specs=(
            pl.BlockSpec((1, STEP, rows_local, NZ), lambda c, i: (part + c, at + i, 0, 0)),
            pl.BlockSpec(
                (devices, None, depth, STEP, width), lambda c, i: (0, c, 0, send_at + i, 0)
            ),
        ),
        out_shape=(
            jax.ShapeDtypeStruct((3, planes, rows_local, NZ), jnp.float32),
            jax.ShapeDtypeStruct((devices, count, depth, send_planes, width), jnp.float32),
        ),
        input_output_aliases=aliases,
        compiler_params=vmem(),
        cost_estimate=cost(
            6 * count * here * STEP * rows_local * NZ * NZ,
            3 * count * here * STEP * rows_local * NZ * 4,
        ),
        name="z_forward",
    )(*operands)


def z_inverse_kernel(received, table, field, low_x, high_x, low_y, high_y):
    rows_local = field.shape[1]
    lines = received.reshape(HALF * STEP, 2 * rows_local)
    pieces = []
    for plane in range(STEP):
        turned = lines[pl.ds(plane, HALF, stride=STEP), :].T
        pieces.append(jnp.concatenate([turned[:rows_local], turned[rows_local:]], axis=1))
    values = times_right(jnp.concatenate(pieces, axis=0), table[...])
    field[...] = values.reshape(STEP, rows_local, NZ)
    low_y[...] = field[:, 0:2, :]
    high_y[...] = field[:, rows_local - 2 : rows_local, :]

    @pl.when(pl.program_id(0) == 0)
    def _():
        low_x[...] = field[0:2]

    @pl.when(pl.program_id(0) == pl.num_programs(0) - 1)
    def _():
        high_x[...] = field[STEP - 2 : STEP]


def z_inverse(received):
    devices, depth, planes, width = received.shape
    rows_local = width // 2
    table = right_table(z_inverse_table())
    layer = pl.BlockSpec((2, rows_local, NZ), lambda i: (0, 0, 0))
    edge = pl.BlockSpec((STEP, 2, NZ), lambda i: (i, 0, 0))
    return pl.pallas_call(
        z_inverse_kernel,
        grid=(planes // STEP,),
        in_specs=[
            pl.BlockSpec((devices, depth, STEP, width), lambda i: (0, 0, i, 0)),
            pl.BlockSpec(table.shape, lambda i: (0, 0)),
        ],
        out_specs=(
            pl.BlockSpec((STEP, rows_local, NZ), lambda i: (i, 0, 0)),
            layer,
            layer,
            edge,
            edge,
        ),
        out_shape=(
            jax.ShapeDtypeStruct((planes, rows_local, NZ), jnp.float32),
            jax.ShapeDtypeStruct((2, rows_local, NZ), jnp.float32),
            jax.ShapeDtypeStruct((2, rows_local, NZ), jnp.float32),
            jax.ShapeDtypeStruct((planes, 2, NZ), jnp.float32),
            jax.ShapeDtypeStruct((planes, 2, NZ), jnp.float32),
        ),
        compiler_params=vmem(),
        cost_estimate=cost(
            6 * planes * rows_local * NZ * NZ, 2 * planes * rows_local * NZ * 4
        ),
        name="z_inverse",
    )(received, table)


def plane_forward_kernel(start, *refs):
    y_table, x_table_ref, spectrum = refs[-3:]
    received = refs[:-3]
    step = pl.program_id(1)
    depth = pl.num_programs(1) - 1
    has_first = start[0] == 0

    @pl.when(jnp.logical_or(step < depth, has_first))
    def _():
        slabs, pens, _, width = received[0].shape
        pieces = []
        for pen in range(pens):
            piece = jnp.concatenate([cells[:, pen] for cells in received], axis=1)
            pieces.append(piece.reshape(slabs * piece.shape[1], width))
        lane = lax.broadcasted_iota(jnp.int32, (1, width), 1)
        real_side = lane < width // 2
        keep_real = jnp.logical_or(real_side, jnp.logical_not(jnp.logical_and(has_first, step == 0)))
        keep_imaginary = jnp.logical_or(jnp.logical_not(real_side), step < depth)
        keep = jnp.logical_and(keep_real, keep_imaginary).astype(jnp.float32)
        lines = jnp.concatenate([piece * keep for piece in pieces], axis=1)
        along_y = times_right(lines, y_table[...])
        rows_y = along_y.shape[1] // 2
        stacked = jnp.concatenate([along_y[:, :rows_y], along_y[:, rows_y:]], axis=0)
        spectrum[...] = times_left(x_table_ref[...], stacked)


def plane_forward(start, received):
    slabs, pens, count, depth, _, width = received[0].shape
    size_x = slabs * sum(cells.shape[4] for cells in received)
    size_y = pens * (width // 2)
    y_table = right_table(y_forward_table(size_y, pens))
    x_matrix = left_table(x_table(size_x, -1.0))
    return pl.pallas_call(
        plane_forward_kernel,
        grid=(count, depth + 1),
        in_specs=[pl.BlockSpec(memory_space=pltpu.SMEM)]
        + [
            pl.BlockSpec(
                (slabs, pens, None, None, cells.shape[4], width),
                lambda c, j: (0, 0, c, jnp.where(j < depth, j, 0), 0, 0),
            )
            for cells in received
        ]
        + [
            pl.BlockSpec(y_table.shape, lambda c, j: (0, 0)),
            pl.BlockSpec(x_matrix.shape, lambda c, j: (0, 0)),
        ],
        out_specs=pl.BlockSpec((None, None, 2 * size_x, size_y), lambda c, j: (c, j, 0, 0)),
        out_shape=jax.ShapeDtypeStruct((count, depth + 1, 2 * size_x, size_y), jnp.float32),
        compiler_params=vmem(),
        cost_estimate=cost(
            24 * count * depth * size_x * size_y * (size_x + size_y),
            4 * count * depth * size_x * size_y * 4,
        ),
        name="plane_forward",
    )(start, *received, y_table, x_matrix)


def wave_pair(shape, dim, length):
    index = lax.broadcasted_iota(jnp.int32, shape, dim)
    signed_index = jnp.where(index < length // 2, index, index - length)
    full_wave = (2.0 * math.pi / length) * signed_index.astype(jnp.float32)
    return full_wave, jnp.where(index == length // 2, 0.0, full_wave)


def plane_inverse_kernel(parts, needs, start, *refs):
    spectra = dict(zip(needs, refs[: len(needs)]))
    extras = dict(zip(needs, refs[len(needs) : 2 * len(needs)]))
    y_table, x_table_ref = refs[2 * len(needs) : 2 * len(needs) + 2]
    backs, turned = refs[2 * len(needs) + 2 : -1], refs[-1]
    step = pl.program_id(0)
    size_x, size_y = turned.shape[1] // 2, turned.shape[2]
    full_x, curl_x = wave_pair((size_x, 1), 0, size_x)
    full_y, curl_y = wave_pair((1, size_y), 1, size_y)

    def curl(part, source, full_z, curl_z):
        curls = (curl_x, curl_y, curl_z)
        wave_left, wave_right = curls[(part + 1) % 3], curls[(part + 2) % 3]
        left, right = source[(part + 1) % 3], source[(part + 2) % 3]
        wave_squared = full_x * full_x + full_y * full_y + full_z * full_z
        present = wave_squared > 0.0
        scaling = jnp.where(present, 1.0 / jnp.where(present, wave_squared, 1.0), 0.0)
        scaling = scaling * (1.0 / float(size_x * size_y * NZ))
        real_part = wave_left * right[:size_x] - wave_right * left[:size_x]
        imaginary = wave_left * right[size_x:] - wave_right * left[size_x:]
        return -imaginary * scaling, real_part * scaling

    index_z = (start[0] + step).astype(jnp.float32)
    wave_z = (2.0 * math.pi / NZ) * index_z
    for at, part in enumerate(parts):
        real_part, imaginary = curl(part, spectra, wave_z, wave_z)
        turned[at, :size_x] = real_part
        turned[at, size_x:] = imaginary

    @pl.when(jnp.logical_and(start[0] == 0, step == 0))
    def _():
        for at, part in enumerate(parts):
            extra_real, extra_imaginary = curl(part, extras, -math.pi, 0.0)
            turned[at, :size_x] += extra_real
            turned[at, size_x:] += extra_imaginary

    slabs, pens, planes, width = backs[0].shape
    for at, back in enumerate(backs):
        along_x = times_left(x_table_ref[...], turned[at])
        lines = jnp.concatenate([along_x[:size_x], along_x[size_x:]], axis=1)
        result = times_right(lines, y_table[...])
        for pen in range(pens):
            piece = result[:, pen * width : (pen + 1) * width]
            back[:, pen] = piece.reshape(slabs, planes, width)


def plane_inverse(parts, start, spectra, shape):
    slabs, pens, depth, planes, width = shape
    count = len(parts)
    size_x = slabs * planes
    size_y = pens * (width // 2)
    y_table = right_table(y_inverse_table(size_y, pens))
    x_matrix = left_table(x_table(size_x, 1.0))
    needs = [c for c in range(3) if any(c != part for part in parts)]

    def at(index, extra):
        return pl.BlockSpec(
            (None, None, 2 * size_x, size_y),
            lambda j: (index, depth if extra else j, 0, 0),
        )

    return pl.pallas_call(
        functools.partial(plane_inverse_kernel, parts, needs),
        grid=(depth,),
        in_specs=[pl.BlockSpec(memory_space=pltpu.SMEM)]
        + [at(spectra[c][1], False) for c in needs]
        + [at(spectra[c][1], True) for c in needs]
        + [
            pl.BlockSpec(y_table.shape, lambda j: (0, 0)),
            pl.BlockSpec(x_matrix.shape, lambda j: (0, 0)),
        ],
        out_specs=[
            pl.BlockSpec((slabs, pens, None, planes, width), lambda j: (0, 0, j, 0, 0))
        ]
        * count,
        out_shape=[jax.ShapeDtypeStruct(shape, jnp.float32)] * count,
        scratch_shapes=[pltpu.VMEM((count, 2 * size_x, size_y), jnp.float32)],
        compiler_params=vmem(),
        cost_estimate=cost(
            24 * count * depth * size_x * size_y * (size_x + size_y),
            6 * count * depth * size_x * size_y * 4,
        ),
        name="plane_inverse",
    )(start, *([spectra[c][0] for c in needs] * 2), y_table, x_matrix)


def z_difference_table():
    table = np.zeros((NZ, NZ), np.float32)
    for cell in range(NZ):
        for shift, weight in ((1, 8.0), (-1, -8.0), (2, -1.0), (-2, 1.0)):
            table[(cell + shift) % NZ, cell] += weight
    table = table.astype(jnp.bfloat16)
    return jnp.asarray(np.concatenate([table, table], axis=0))


def stretch_kernel(vorticity, field, before, after, low_x, high_x, low_y, high_y, table, *refs):
    velocity, stretching, padded = refs[-3:]
    step = pl.program_id(0)
    rows_local = field.shape[1]
    first = step == 0
    last = step == pl.num_programs(0) - 1
    own = slice(8, 8 + rows_local)
    for plane in range(STEP):
        padded[plane, own, :] = field[plane]
        padded[plane, 6:8, :] = low_y[plane]
        padded[plane, 8 + rows_local : 10 + rows_local, :] = high_y[plane]
    high, low = split_values(field[...].reshape(STEP * rows_local, NZ))
    along_z = jnp.dot(
        jnp.concatenate([high, low], axis=1), table[...], preferred_element_type=jnp.float32
    )

    def difference(ahead, behind, ahead_2, behind_2):
        return 8.0 * (ahead - behind) - (ahead_2 - behind_2)

    def along(plane):
        if plane < 0:
            return jnp.where(first, low_x[plane + 2], before[plane + 2])
        if plane >= STEP:
            return jnp.where(last, high_x[plane - STEP], after[plane - STEP])
        return field[plane]

    for plane in range(STEP):
        velocity[0, plane] = field[plane]
        along_x = difference(*(along(plane + shift) for shift in (1, -1, 2, -2)))
        along_y = difference(
            *(padded[plane, 8 + shift : 8 + shift + rows_local, :] for shift in (1, -1, 2, -2))
        )
        total = vorticity[0, plane] * along_x + vorticity[1, plane] * along_y
        total = total + vorticity[2, plane] * along_z[plane * rows_local : (plane + 1) * rows_local]
        stretching[0, plane] = total * (1.0 / 12.0)


def stretch(part, vorticity, field, halos, outputs):
    planes, rows_local, _ = field.shape
    pairs = STEP // 2
    table = z_difference_table()
    layer = pl.BlockSpec((2, rows_local, NZ), lambda i: (0, 0, 0))
    edge = pl.BlockSpec((STEP, 2, NZ), lambda i: (i, 0, 0))
    block = pl.BlockSpec((1, STEP, rows_local, NZ), lambda i: (part, i, 0, 0))
    specs = [
        pl.BlockSpec((3, STEP, rows_local, NZ), lambda i: (0, i, 0, 0)),
        pl.BlockSpec((STEP, rows_local, NZ), lambda i: (i, 0, 0)),
        pl.BlockSpec((2, rows_local, NZ), lambda i: (jnp.maximum(i * pairs - 1, 0), 0, 0)),
        pl.BlockSpec(
            (2, rows_local, NZ), lambda i: (jnp.minimum((i + 1) * pairs, planes // 2 - 1), 0, 0)
        ),
        layer,
        layer,
        edge,
        edge,
        pl.BlockSpec(table.shape, lambda i: (0, 0)),
    ]
    operands = [vorticity, field, field, field, *halos, table]
    aliases = {}
    if outputs is not None:
        aliases = {len(operands): 0, len(operands) + 1: 1}
        specs += [pl.BlockSpec(memory_space=pl.ANY)] * 2
        operands += list(outputs)
    shape = jax.ShapeDtypeStruct((3, planes, rows_local, NZ), jnp.float32)
    return pl.pallas_call(
        stretch_kernel,
        grid=(planes // STEP,),
        in_specs=specs,
        out_specs=(block, block),
        out_shape=(shape, shape),
        input_output_aliases=aliases,
        scratch_shapes=[pltpu.VMEM((STEP, rows_local + 16, NZ), jnp.float32)],
        compiler_params=vmem(),
        cost_estimate=cost(600 * planes * rows_local * NZ, 7 * planes * rows_local * NZ * 4),
        name="stretch",
    )(*operands)


def per_device(counts, row_base, z_base, fractions, strength):
    slabs, pens = lax.axis_size("slab"), lax.axis_size("pen")
    devices = slabs * pens
    depth = HALF // devices
    planes, blocks, _ = row_base.shape
    rows_local = blocks * BLOCK_ROWS
    width = 2 * rows_local
    place = lax.axis_index("slab") * pens + lax.axis_index("pen")
    start = (place * depth).astype(jnp.int32).reshape(1)
    shape = (devices, depth, planes, width)

    def exchange(blocks_out, after=None):
        if after is not None:
            blocks_out, _ = lax.optimization_barrier((blocks_out, after))
        return lax.all_to_all(blocks_out, AXES, 0, 0, tiled=True)

    def unfold(received):
        return received.reshape((slabs, pens) + received.shape[1:])

    cut = (planes // STEP // 2) * STEP
    particles = (counts, row_base, z_base, fractions, strength)
    grid, ghost_y, ghost_x, ghost_xy = deposit(particles, cut, planes)
    tail = (grid, next_over(ghost_y, ("pen",)))
    ghosts_x = (next_over(ghost_x, ("slab",)), next_over(ghost_xy, ("slab", "pen")))
    everything = (cut, planes)
    if cut == 0:
        vorticity, send = z_forward((1, 2), everything, tail, ghosts_x, None, None, shape)
        received = [exchange(send)]
        vorticity, send = z_forward((0,), everything, tail, ghosts_x, vorticity, None, shape)
    else:
        vorticity, send = z_forward((1, 2), everything, tail, None, None, None, shape)
        held, _ = lax.optimization_barrier((particles, send))
        grid, ghost_y = deposit(held, 0, cut)
        head = (grid, next_over(ghost_y, ("pen",)))
        received = [exchange(send)]
        vorticity, send = z_forward((1, 2), (0, cut), head, ghosts_x, vorticity, None, shape)
        received = [exchange(send, received[0])] + received
        vorticity, send = z_forward((0,), (0, cut), head, ghosts_x, vorticity, NEW, shape)
        vorticity, send = z_forward((0,), everything, tail, None, vorticity, send, shape)
    pair = plane_forward(start, [unfold(cells) for cells in received])
    single = plane_forward(start, [unfold(exchange(send, received[0]))])
    spectra = {1: (pair, 0), 2: (pair, 1), 0: (single, 0)}

    shape = (slabs, pens, depth, planes, width)
    backs = plane_inverse((0,), start, spectra, shape) + plane_inverse((1, 2), start, spectra, shape)
    outputs = received = None
    layers = []
    for part, back in enumerate(backs):
        back = back.reshape(devices, depth, planes, width)
        received = exchange(back, None if part == 0 else (received, layers[: part - 1]))
        if part == 2:
            received, outputs = lax.optimization_barrier((received, outputs))
        field, low_x, high_x, low_y, high_y = z_inverse(received)
        halos = (
            shifted(high_x, "slab", 1),
            shifted(low_x, "slab", -1),
            shifted(high_y, "pen", 1),
            shifted(low_y, "pen", -1),
        )
        layers.append(halos)
        outputs = stretch(part, vorticity, field, halos, outputs)
    return (vorticity, outputs[0], outputs[1])


def solution(mesh):
    in_specs = (
        P("slab", "pen"),
        P("slab", "pen", None),
        P("slab", "pen", None),
        P(None, "slab", "pen", None),
        P(None, "slab", "pen", None),
    )
    out_specs = (
        P(None, "slab", "pen", None),
        P(None, "slab", "pen", None),
        P(None, "slab", "pen", None),
    )
    return jax.shard_map(
        per_device, mesh=mesh, in_specs=in_specs, out_specs=out_specs, check_vma=False
    )
```

```python
import functools
import math

import jax
import jax.numpy as jnp
import numpy as np
from jax import lax
from jax.experimental import pallas as pl
from jax.experimental.pallas import tpu as pltpu
from jax.sharding import PartitionSpec as P

NZ = 256
BLOCK_ROWS = 16
HALF = NZ // 2
STEP = 8
SLOTS_AT_ONCE = 256
MIB = 1024 * 1024
NEW = object()
AXES = ("slab", "pen")


def kernel_weight(distance):
    magnitude = jnp.abs(distance)
    inner_part = 1.0 - 2.5 * magnitude * magnitude + 1.5 * magnitude * magnitude * magnitude
    outer_part = 0.5 * (2.0 - magnitude) * (2.0 - magnitude) * (1.0 - magnitude)
    return jnp.where(magnitude < 1.0, inner_part, jnp.where(magnitude < 2.0, outer_part, 0.0))


def vmem(limit=48, **extra):
    return pltpu.CompilerParams(vmem_limit_bytes=limit * MIB, **extra)


def cost(flops, moved):
    return pl.CostEstimate(flops=int(flops), bytes_accessed=int(moved), transcendentals=0)


def two_parts(table):
    table = np.asarray(table, np.float32)
    high = table.astype(jnp.bfloat16)
    low = (table - high.astype(np.float32)).astype(jnp.bfloat16)
    return high, low


def right_table(table):
    high, low = two_parts(table)
    return jnp.asarray(np.concatenate([high, high, low], axis=0))


def left_table(table):
    high, low = two_parts(table)
    return jnp.asarray(np.concatenate([high, high, low], axis=1))


def waves(length):
    index = np.arange(length)
    angle = 2.0 * np.pi / length * (index[:, None] * index[None, :] % length)
    return np.cos(angle), np.sin(angle)


def z_forward_table():
    cosine, sine = waves(NZ)
    real_part, imaginary = cosine[:, :HALF].copy(), -sine[:, :HALF]
    imaginary[:, 0] = cosine[:, HALF]
    return np.concatenate([real_part, imaginary], axis=1)


def z_inverse_table():
    cosine, sine = waves(NZ)
    real_part, imaginary = 2.0 * cosine[:HALF], -2.0 * sine[:HALF]
    real_part[0] = 1.0
    imaginary[0] = cosine[HALF]
    return np.concatenate([real_part, imaginary], axis=0)


def y_forward_table(length, parts):
    cosine, sine = waves(length)
    width = length // parts
    rows = []
    for part in range(parts):
        here = slice(part * width, (part + 1) * width)
        rows.append(np.concatenate([cosine[here], -sine[here]], axis=1))
        rows.append(np.concatenate([sine[here], cosine[here]], axis=1))
    return np.concatenate(rows, axis=0)


def y_inverse_table(length, parts):
    cosine, sine = waves(length)
    width = length // parts
    columns = []
    for part in range(parts):
        here = slice(part * width, (part + 1) * width)
        columns.append(np.concatenate([cosine[:, here], -sine[:, here]], axis=0))
        columns.append(np.concatenate([sine[:, here], cosine[:, here]], axis=0))
    return np.concatenate(columns, axis=1)


def x_table(length, sign):
    cosine, sine = waves(length)
    return np.concatenate(
        [
            np.concatenate([cosine, -sign * sine], axis=1),
            np.concatenate([sign * sine, cosine], axis=1),
        ],
        axis=0,
    )


def split_values(values):
    high = values.astype(jnp.bfloat16)
    low = (values - high.astype(jnp.float32)).astype(jnp.bfloat16)
    return high, low


def times_right(values, table):
    high, low = split_values(values)
    return jnp.dot(
        jnp.concatenate([high, low, high], axis=1), table, preferred_element_type=jnp.float32
    )


def times_left(table, values):
    high, low = split_values(values)
    return jnp.dot(
        table, jnp.concatenate([high, low, high], axis=0), preferred_element_type=jnp.float32
    )


def deposit_kernel(begin, end, counts, row_base, z_base, fractions, strength, *refs):
    planes, blocks, slots = row_base.shape
    first_source = max(begin - 3, 0)
    last = end == planes
    width = min(SLOTS_AT_ONCE, slots)
    rows_local = blocks * BLOCK_ROWS
    ext = BLOCK_ROWS + 8
    if last:
        grid, ghost_y, ghost_x, ghost_xy = refs[:4]
    else:
        grid, ghost_y = refs[:2]
    rows, row_here, z_here, fractions_here, strength_here, arrived = refs[-6:]
    taken = slice(first_source, end)
    copies = [
        pltpu.make_async_copy(row_base.at[taken], row_here, arrived.at[0]),
        pltpu.make_async_copy(z_base.at[taken], z_here, arrived.at[1]),
        pltpu.make_async_copy(fractions.at[:, taken], fractions_here, arrived.at[2]),
        pltpu.make_async_copy(strength.at[:, taken], strength_here, arrived.at[3]),
    ]
    for copy in copies:
        copy.start()

    def clear(plane, _):
        grid[:, plane] = jnp.zeros((3,) + grid.shape[2:], jnp.float32)
        return 0

    lax.fori_loop(0, grid.shape[1], clear, 0)
    z_rows = 16
    z_iota = lax.broadcasted_iota(jnp.int32, (z_rows, width), 0)
    j_iota = lax.broadcasted_iota(jnp.int32, (ext, width), 0).astype(jnp.float32)
    z_tiles = [
        (z_iota + z_rows * t).astype(jnp.float32).astype(jnp.bfloat16) for t in range(NZ // z_rows)
    ]
    for copy in copies:
        copy.wait()

    def one_plane(offsets, source, _):
        plane = source + first_source
        slot = lax.broadcasted_iota(jnp.int32, (blocks, slots), 1)
        group = lax.broadcasted_iota(jnp.int32, (blocks, slots), 0)
        count = jnp.zeros((blocks, slots), jnp.int32)
        for block in range(blocks):
            count = jnp.where(group == block, counts[plane, block], count)
        live = slot < count
        row_cell = row_here[source].astype(jnp.float32)
        z_cell = z_here[source]
        for offset in range(4):
            weight_x = kernel_weight(float(offset - 1) - fractions_here[0, source])
            for part in range(3):
                rows[part * 4 + offset] = jnp.where(live, strength_here[part, source] * weight_x, 0.0)
            rows[12 + offset] = kernel_weight(float(offset - 1) - fractions_here[1, source])
            rows[16 + offset] = row_cell + float(offset)
            rows[20 + offset] = kernel_weight(float(offset - 1) - fractions_here[2, source])
            rows[24 + offset] = jnp.bitwise_and(z_cell + offset, NZ - 1).astype(jnp.float32)

        used = [(part, offset) for part in range(3) for offset in offsets]

        def spread(block, first):
            here = slice(first, first + width)

            def row(index):
                return rows[index, block : block + 1, here]

            weight_y = jnp.zeros((ext, width), jnp.float32)
            for offset in range(4):
                weight_y = jnp.where(j_iota == row(16 + offset), row(12 + offset), weight_y)
            coefs = jnp.concatenate([row(p * 4 + o) * weight_y for p, o in used], axis=0)
            coefs = coefs.astype(jnp.bfloat16)
            z_weight = [
                jnp.broadcast_to(row(20 + offset), (z_rows, width)).astype(jnp.bfloat16)
                for offset in range(4)
            ]
            z_place = [
                jnp.broadcast_to(row(24 + offset), (z_rows, width)).astype(jnp.bfloat16)
                for offset in range(4)
            ]
            tiles = []
            for z_tile in z_tiles:
                tile = jnp.zeros((z_rows, width), jnp.bfloat16)
                for offset in range(4):
                    tile = jnp.where(z_tile == z_place[offset], z_weight[offset], tile)
                tiles.append(tile)
            weight_z = jnp.concatenate(tiles, axis=0)
            result = lax.dot_general(
                coefs, weight_z, (((1,), (1,)), ((), ())), preferred_element_type=jnp.float32
            )
            low = block * BLOCK_ROWS
            for index, (part, offset) in enumerate(used):
                grid[part, plane + offset - begin, low : low + ext, :] += result[
                    index * ext : (index + 1) * ext
                ]

        for block in range(blocks):
            spread(block, 0)
        for first in range(width, slots, width):
            for block in range(blocks):
                pl.when(counts[plane, block] > first)(functools.partial(spread, block, first))
        return 0

    top = end + 3 if last else end
    inner_begin, inner_end = begin, top - 3
    for plane in range(first_source, begin):
        offsets = [o for o in range(4) if begin <= plane + o]
        one_plane(offsets, plane - first_source, 0)
    lax.fori_loop(
        inner_begin - first_source,
        inner_end - first_source,
        functools.partial(one_plane, list(range(4))),
        0,
    )
    for plane in range(inner_end, end):
        offsets = [o for o in range(4) if plane + o < top]
        one_plane(offsets, plane - first_source, 0)

    def side(plane, _):
        ghost_y[:, plane] = grid[:, plane, rows_local : rows_local + 3, :]
        return 0

    lax.fori_loop(0, end - begin, side, 0)
    if last:
        for part in range(3):
            for offset in range(3):
                plane = end - begin + offset
                ghost_x[part, offset] = grid[part, plane, :rows_local, :]
                ghost_xy[part, offset] = grid[part, plane, rows_local : rows_local + 3, :]


def deposit(particles, begin, end):
    planes, blocks, slots = particles[1].shape
    sources = end - max(begin - 3, 0)
    rows_local = blocks * BLOCK_ROWS
    whole = pl.BlockSpec(memory_space=pltpu.VMEM)
    last = end == planes
    shapes = [(3, end - begin + (3 if last else 0), rows_local + 8, NZ), (3, end - begin, 3, NZ)]
    if last:
        shapes += [(3, 3, rows_local, NZ), (3, 3, 3, NZ)]
    return pl.pallas_call(
        functools.partial(deposit_kernel, begin, end),
        out_shape=[jax.ShapeDtypeStruct(shape, jnp.float32) for shape in shapes],
        in_specs=[pl.BlockSpec(memory_space=pltpu.SMEM)]
        + [pl.BlockSpec(memory_space=pltpu.HBM)] * 4,
        out_specs=[whole] * len(shapes),
        scratch_shapes=[
            pltpu.VMEM((28, blocks, slots), jnp.float32),
            pltpu.VMEM((sources, blocks, slots), jnp.int32),
            pltpu.VMEM((sources, blocks, slots), jnp.int32),
            pltpu.VMEM((3, sources, blocks, slots), jnp.float32),
            pltpu.VMEM((3, sources, blocks, slots), jnp.float32),
            pltpu.SemaphoreType.DMA((4,)),
        ],
        compiler_params=vmem(),
        cost_estimate=cost(10 * sources * blocks * 288 * slots * NZ, 12 * MIB),
        name="deposit",
    )(*particles)


def next_over(block, axes):
    counts = [lax.axis_size(axis) for axis in AXES]
    route = []
    for slab in range(counts[0]):
        for pen in range(counts[1]):
            to_slab = (slab + 1) % counts[0] if "slab" in axes else slab
            to_pen = (pen + 1) % counts[1] if "pen" in axes else pen
            route.append((slab * counts[1] + pen, to_slab * counts[1] + to_pen))
    return lax.ppermute(block, AXES, route)


def shifted(block, axis, distance):
    count = lax.axis_size(axis)
    return lax.ppermute(block, axis, [(i, (i + distance) % count) for i in range(count)])


def z_forward_body(with_x, grid, ghost_y, *refs):
    vorticity, send = refs[-2:]
    table = refs[-3]
    rows_local = vorticity.shape[2]
    vorticity[0] = grid[0, :, :rows_local, :]
    vorticity[0, :, 0:3, :] += ghost_y[0]
    if with_x:
        ghost_x, ghost_xy = refs[:2]

        @pl.when(pl.program_id(1) == 0)
        def _():
            vorticity[0, 0:3] += ghost_x[0]
            vorticity[0, 0:3, 0:3, :] += ghost_xy[0]

    spectrum = times_right(vorticity[0].reshape(STEP * rows_local, NZ), table[...])
    lines = send.reshape(HALF * STEP, 2 * rows_local)
    for plane in range(STEP):
        here = spectrum[plane * rows_local : (plane + 1) * rows_local]
        stacked = jnp.concatenate([here[:, :HALF], here[:, HALF:]], axis=0)
        lines[pl.ds(plane, HALF, stride=STEP), :] = stacked.T


def z_forward(parts, cell_range, deposited, ghosts_x, vorticity, send, shape):
    devices, depth, planes, width = shape
    begin, end = cell_range
    grid, ghost_y = deposited
    rows_local = width // 2
    count = len(parts)
    part = parts[0]
    table = right_table(z_forward_table())
    here = (end - begin) // STEP
    at = begin // STEP
    joined = send is not None
    send_at = at if joined else 0
    send_planes = planes if joined else end - begin
    specs = [
        pl.BlockSpec((1, STEP, rows_local + 8, NZ), lambda c, i: (part + c, i, 0, 0)),
        pl.BlockSpec((1, STEP, 3, NZ), lambda c, i: (part + c, i, 0, 0)),
    ]
    operands = [grid, ghost_y]
    if ghosts_x is not None:
        operands += list(ghosts_x)
        specs += [
            pl.BlockSpec((1, 3, rows_local, NZ), lambda c, i: (part + c, 0, 0, 0)),
            pl.BlockSpec((1, 3, 3, NZ), lambda c, i: (part + c, 0, 0, 0)),
        ]
    operands.append(table)
    specs.append(pl.BlockSpec(table.shape, lambda c, i: (0, 0)))
    aliases = {}
    for index, output in enumerate((vorticity, send)):
        if output is not None and output is not NEW:
            aliases[len(operands)] = index
            specs.append(pl.BlockSpec(memory_space=pl.ANY))
            operands.append(output)
    used = 5 if ghosts_x is not None else 3

    def kernel(*refs):
        z_forward_body(ghosts_x is not None, *refs[:used], *refs[-2:])

    return pl.pallas_call(
        kernel,
        grid=(count, here),
        in_specs=specs,
        out_specs=(
            pl.BlockSpec((1, STEP, rows_local, NZ), lambda c, i: (part + c, at + i, 0, 0)),
            pl.BlockSpec(
                (devices, None, depth, STEP, width), lambda c, i: (0, c, 0, send_at + i, 0)
            ),
        ),
        out_shape=(
            jax.ShapeDtypeStruct((3, planes, rows_local, NZ), jnp.float32),
            jax.ShapeDtypeStruct((devices, count, depth, send_planes, width), jnp.float32),
        ),
        input_output_aliases=aliases,
        compiler_params=vmem(),
        cost_estimate=cost(
            6 * count * here * STEP * rows_local * NZ * NZ,
            3 * count * here * STEP * rows_local * NZ * 4,
        ),
        name="z_forward",
    )(*operands)


def z_inverse_kernel(received, table, field, low_x, high_x, low_y, high_y):
    rows_local = field.shape[1]
    lines = received.reshape(HALF * STEP, 2 * rows_local)
    pieces = []
    for plane in range(STEP):
        turned = lines[pl.ds(plane, HALF, stride=STEP), :].T
        pieces.append(jnp.concatenate([turned[:rows_local], turned[rows_local:]], axis=1))
    values = times_right(jnp.concatenate(pieces, axis=0), table[...])
    field[...] = values.reshape(STEP, rows_local, NZ)
    low_y[...] = field[:, 0:2, :]
    high_y[...] = field[:, rows_local - 2 : rows_local, :]

    @pl.when(pl.program_id(0) == 0)
    def _():
        low_x[...] = field[0:2]

    @pl.when(pl.program_id(0) == pl.num_programs(0) - 1)
    def _():
        high_x[...] = field[STEP - 2 : STEP]


def z_inverse(received):
    devices, depth, planes, width = received.shape
    rows_local = width // 2
    table = right_table(z_inverse_table())
    layer = pl.BlockSpec((2, rows_local, NZ), lambda i: (0, 0, 0))
    edge = pl.BlockSpec((STEP, 2, NZ), lambda i: (i, 0, 0))
    return pl.pallas_call(
        z_inverse_kernel,
        grid=(planes // STEP,),
        in_specs=[
            pl.BlockSpec((devices, depth, STEP, width), lambda i: (0, 0, i, 0)),
            pl.BlockSpec(table.shape, lambda i: (0, 0)),
        ],
        out_specs=(
            pl.BlockSpec((STEP, rows_local, NZ), lambda i: (i, 0, 0)),
            layer,
            layer,
            edge,
            edge,
        ),
        out_shape=(
            jax.ShapeDtypeStruct((planes, rows_local, NZ), jnp.float32),
            jax.ShapeDtypeStruct((2, rows_local, NZ), jnp.float32),
            jax.ShapeDtypeStruct((2, rows_local, NZ), jnp.float32),
            jax.ShapeDtypeStruct((planes, 2, NZ), jnp.float32),
            jax.ShapeDtypeStruct((planes, 2, NZ), jnp.float32),
        ),
        compiler_params=vmem(),
        cost_estimate=cost(
            6 * planes * rows_local * NZ * NZ, 2 * planes * rows_local * NZ * 4
        ),
        name="z_inverse",
    )(received, table)


def plane_forward_kernel(start, *refs):
    y_table, x_table_ref, spectrum = refs[-3:]
    received = refs[:-3]
    step = pl.program_id(1)
    depth = pl.num_programs(1) - 1
    has_first = start[0] == 0

    @pl.when(jnp.logical_or(step < depth, has_first))
    def _():
        slabs, pens, _, width = received[0].shape
        pieces = []
        for pen in range(pens):
            piece = jnp.concatenate([cells[:, pen] for cells in received], axis=1)
            pieces.append(piece.reshape(slabs * piece.shape[1], width))
        lane = lax.broadcasted_iota(jnp.int32, (1, width), 1)
        real_side = lane < width // 2
        keep_real = jnp.logical_or(real_side, jnp.logical_not(jnp.logical_and(has_first, step == 0)))
        keep_imaginary = jnp.logical_or(jnp.logical_not(real_side), step < depth)
        keep = jnp.logical_and(keep_real, keep_imaginary).astype(jnp.float32)
        lines = jnp.concatenate([piece * keep for piece in pieces], axis=1)
        along_y = times_right(lines, y_table[...])
        rows_y = along_y.shape[1] // 2
        stacked = jnp.concatenate([along_y[:, :rows_y], along_y[:, rows_y:]], axis=0)
        spectrum[...] = times_left(x_table_ref[...], stacked)


def plane_forward(start, received):
    slabs, pens, count, depth, _, width = received[0].shape
    size_x = slabs * sum(cells.shape[4] for cells in received)
    size_y = pens * (width // 2)
    y_table = right_table(y_forward_table(size_y, pens))
    x_matrix = left_table(x_table(size_x, -1.0))
    return pl.pallas_call(
        plane_forward_kernel,
        grid=(count, depth + 1),
        in_specs=[pl.BlockSpec(memory_space=pltpu.SMEM)]
        + [
            pl.BlockSpec(
                (slabs, pens, None, None, cells.shape[4], width),
                lambda c, j: (0, 0, c, jnp.where(j < depth, j, 0), 0, 0),
            )
            for cells in received
        ]
        + [
            pl.BlockSpec(y_table.shape, lambda c, j: (0, 0)),
            pl.BlockSpec(x_matrix.shape, lambda c, j: (0, 0)),
        ],
        out_specs=pl.BlockSpec((None, None, 2 * size_x, size_y), lambda c, j: (c, j, 0, 0)),
        out_shape=jax.ShapeDtypeStruct((count, depth + 1, 2 * size_x, size_y), jnp.float32),
        compiler_params=vmem(),
        cost_estimate=cost(
            24 * count * depth * size_x * size_y * (size_x + size_y),
            4 * count * depth * size_x * size_y * 4,
        ),
        name="plane_forward",
    )(start, *received, y_table, x_matrix)


def wave_pair(shape, dim, length):
    index = lax.broadcasted_iota(jnp.int32, shape, dim)
    signed_index = jnp.where(index < length // 2, index, index - length)
    full_wave = (2.0 * math.pi / length) * signed_index.astype(jnp.float32)
    return full_wave, jnp.where(index == length // 2, 0.0, full_wave)


def plane_inverse_kernel(parts, needs, start, *refs):
    spectra = dict(zip(needs, refs[: len(needs)]))
    extras = dict(zip(needs, refs[len(needs) : 2 * len(needs)]))
    y_table, x_table_ref = refs[2 * len(needs) : 2 * len(needs) + 2]
    backs, turned = refs[2 * len(needs) + 2 : -1], refs[-1]
    step = pl.program_id(0)
    size_x, size_y = turned.shape[1] // 2, turned.shape[2]
    full_x, curl_x = wave_pair((size_x, 1), 0, size_x)
    full_y, curl_y = wave_pair((1, size_y), 1, size_y)

    def curl(part, source, full_z, curl_z):
        curls = (curl_x, curl_y, curl_z)
        wave_left, wave_right = curls[(part + 1) % 3], curls[(part + 2) % 3]
        left, right = source[(part + 1) % 3], source[(part + 2) % 3]
        wave_squared = full_x * full_x + full_y * full_y + full_z * full_z
        present = wave_squared > 0.0
        scaling = jnp.where(present, 1.0 / jnp.where(present, wave_squared, 1.0), 0.0)
        scaling = scaling * (1.0 / float(size_x * size_y * NZ))
        real_part = wave_left * right[:size_x] - wave_right * left[:size_x]
        imaginary = wave_left * right[size_x:] - wave_right * left[size_x:]
        return -imaginary * scaling, real_part * scaling

    index_z = (start[0] + step).astype(jnp.float32)
    wave_z = (2.0 * math.pi / NZ) * index_z
    for at, part in enumerate(parts):
        real_part, imaginary = curl(part, spectra, wave_z, wave_z)
        turned[at, :size_x] = real_part
        turned[at, size_x:] = imaginary

    @pl.when(jnp.logical_and(start[0] == 0, step == 0))
    def _():
        for at, part in enumerate(parts):
            extra_real, extra_imaginary = curl(part, extras, -math.pi, 0.0)
            turned[at, :size_x] += extra_real
            turned[at, size_x:] += extra_imaginary

    slabs, pens, planes, width = backs[0].shape
    for at, back in enumerate(backs):
        along_x = times_left(x_table_ref[...], turned[at])
        lines = jnp.concatenate([along_x[:size_x], along_x[size_x:]], axis=1)
        result = times_right(lines, y_table[...])
        for pen in range(pens):
            piece = result[:, pen * width : (pen + 1) * width]
            back[:, pen] = piece.reshape(slabs, planes, width)


def plane_inverse(parts, start, spectra, shape):
    slabs, pens, depth, planes, width = shape
    count = len(parts)
    size_x = slabs * planes
    size_y = pens * (width // 2)
    y_table = right_table(y_inverse_table(size_y, pens))
    x_matrix = left_table(x_table(size_x, 1.0))
    needs = [c for c in range(3) if any(c != part for part in parts)]

    def at(index, extra):
        return pl.BlockSpec(
            (None, None, 2 * size_x, size_y),
            lambda j: (index, depth if extra else j, 0, 0),
        )

    return pl.pallas_call(
        functools.partial(plane_inverse_kernel, parts, needs),
        grid=(depth,),
        in_specs=[pl.BlockSpec(memory_space=pltpu.SMEM)]
        + [at(spectra[c][1], False) for c in needs]
        + [at(spectra[c][1], True) for c in needs]
        + [
            pl.BlockSpec(y_table.shape, lambda j: (0, 0)),
            pl.BlockSpec(x_matrix.shape, lambda j: (0, 0)),
        ],
        out_specs=[
            pl.BlockSpec((slabs, pens, None, planes, width), lambda j: (0, 0, j, 0, 0))
        ]
        * count,
        out_shape=[jax.ShapeDtypeStruct(shape, jnp.float32)] * count,
        scratch_shapes=[pltpu.VMEM((count, 2 * size_x, size_y), jnp.float32)],
        compiler_params=vmem(),
        cost_estimate=cost(
            24 * count * depth * size_x * size_y * (size_x + size_y),
            6 * count * depth * size_x * size_y * 4,
        ),
        name="plane_inverse",
    )(start, *([spectra[c][0] for c in needs] * 2), y_table, x_matrix)


def z_difference_table():
    table = np.zeros((NZ, NZ), np.float32)
    for cell in range(NZ):
        for shift, weight in ((1, 8.0), (-1, -8.0), (2, -1.0), (-2, 1.0)):
            table[(cell + shift) % NZ, cell] += weight
    table = table.astype(jnp.bfloat16)
    return jnp.asarray(np.concatenate([table, table], axis=0))


def stretch_kernel(vorticity, field, before, after, low_x, high_x, low_y, high_y, table, *refs):
    velocity, stretching, padded = refs[-3:]
    step = pl.program_id(0)
    rows_local = field.shape[1]
    first = step == 0
    last = step == pl.num_programs(0) - 1
    own = slice(8, 8 + rows_local)
    for plane in range(STEP):
        padded[plane, own, :] = field[plane]
        padded[plane, 6:8, :] = low_y[plane]
        padded[plane, 8 + rows_local : 10 + rows_local, :] = high_y[plane]
    high, low = split_values(field[...].reshape(STEP * rows_local, NZ))
    along_z = jnp.dot(
        jnp.concatenate([high, low], axis=1), table[...], preferred_element_type=jnp.float32
    )

    def difference(ahead, behind, ahead_2, behind_2):
        return 8.0 * (ahead - behind) - (ahead_2 - behind_2)

    def along(plane):
        if plane < 0:
            return jnp.where(first, low_x[plane + 2], before[plane + 2])
        if plane >= STEP:
            return jnp.where(last, high_x[plane - STEP], after[plane - STEP])
        return field[plane]

    for plane in range(STEP):
        velocity[0, plane] = field[plane]
        along_x = difference(*(along(plane + shift) for shift in (1, -1, 2, -2)))
        along_y = difference(
            *(padded[plane, 8 + shift : 8 + shift + rows_local, :] for shift in (1, -1, 2, -2))
        )
        total = vorticity[0, plane] * along_x + vorticity[1, plane] * along_y
        total = total + vorticity[2, plane] * along_z[plane * rows_local : (plane + 1) * rows_local]
        stretching[0, plane] = total * (1.0 / 12.0)


def stretch(part, vorticity, field, halos, outputs):
    planes, rows_local, _ = field.shape
    pairs = STEP // 2
    table = z_difference_table()
    layer = pl.BlockSpec((2, rows_local, NZ), lambda i: (0, 0, 0))
    edge = pl.BlockSpec((STEP, 2, NZ), lambda i: (i, 0, 0))
    block = pl.BlockSpec((1, STEP, rows_local, NZ), lambda i: (part, i, 0, 0))
    specs = [
        pl.BlockSpec((3, STEP, rows_local, NZ), lambda i: (0, i, 0, 0)),
        pl.BlockSpec((STEP, rows_local, NZ), lambda i: (i, 0, 0)),
        pl.BlockSpec((2, rows_local, NZ), lambda i: (jnp.maximum(i * pairs - 1, 0), 0, 0)),
        pl.BlockSpec(
            (2, rows_local, NZ), lambda i: (jnp.minimum((i + 1) * pairs, planes // 2 - 1), 0, 0)
        ),
        layer,
        layer,
        edge,
        edge,
        pl.BlockSpec(table.shape, lambda i: (0, 0)),
    ]
    operands = [vorticity, field, field, field, *halos, table]
    aliases = {}
    if outputs is not None:
        aliases = {len(operands): 0, len(operands) + 1: 1}
        specs += [pl.BlockSpec(memory_space=pl.ANY)] * 2
        operands += list(outputs)
    shape = jax.ShapeDtypeStruct((3, planes, rows_local, NZ), jnp.float32)
    return pl.pallas_call(
        stretch_kernel,
        grid=(planes // STEP,),
        in_specs=specs,
        out_specs=(block, block),
        out_shape=(shape, shape),
        input_output_aliases=aliases,
        scratch_shapes=[pltpu.VMEM((STEP, rows_local + 16, NZ), jnp.float32)],
        compiler_params=vmem(),
        cost_estimate=cost(600 * planes * rows_local * NZ, 7 * planes * rows_local * NZ * 4),
        name="stretch",
    )(*operands)


def per_device(counts, row_base, z_base, fractions, strength):
    slabs, pens = lax.axis_size("slab"), lax.axis_size("pen")
    devices = slabs * pens
    depth = HALF // devices
    planes, blocks, _ = row_base.shape
    rows_local = blocks * BLOCK_ROWS
    width = 2 * rows_local
    place = lax.axis_index("slab") * pens + lax.axis_index("pen")
    start = (place * depth).astype(jnp.int32).reshape(1)
    shape = (devices, depth, planes, width)

    def exchange(blocks_out, after=None):
        if after is not None:
            blocks_out, _ = lax.optimization_barrier((blocks_out, after))
        return lax.all_to_all(blocks_out, AXES, 0, 0, tiled=True)

    def unfold(received):
        return received.reshape((slabs, pens) + received.shape[1:])

    cut = planes - STEP
    particles = (counts, row_base, z_base, fractions, strength)
    grid, ghost_y, ghost_x, ghost_xy = deposit(particles, cut, planes)
    tail = (grid, next_over(ghost_y, ("pen",)))
    ghosts_x = (next_over(ghost_x, ("slab",)), next_over(ghost_xy, ("slab", "pen")))
    everything = (cut, planes)
    if cut == 0:
        vorticity, send = z_forward((1, 2), everything, tail, ghosts_x, None, None, shape)
        received = [exchange(send)]
        vorticity, send = z_forward((0,), everything, tail, ghosts_x, vorticity, None, shape)
    else:
        vorticity, send = z_forward((1, 2), everything, tail, None, None, None, shape)
        held, _ = lax.optimization_barrier((particles, send))
        grid, ghost_y = deposit(held, 0, cut)
        head = (grid, next_over(ghost_y, ("pen",)))
        received = [exchange(send)]
        vorticity, send = z_forward((1, 2), (0, cut), head, ghosts_x, vorticity, None, shape)
        received = [exchange(send, received[0])] + received
        vorticity, send = z_forward((0,), (0, cut), head, ghosts_x, vorticity, NEW, shape)
        vorticity, send = z_forward((0,), everything, tail, None, vorticity, send, shape)
    pair = plane_forward(start, [unfold(cells) for cells in received])
    single = plane_forward(start, [unfold(exchange(send, received[0]))])
    spectra = {1: (pair, 0), 2: (pair, 1), 0: (single, 0)}

    shape = (slabs, pens, depth, planes, width)
    backs = plane_inverse((0,), start, spectra, shape) + plane_inverse((1, 2), start, spectra, shape)
    outputs = received = None
    layers = []
    for part, back in enumerate(backs):
        back = back.reshape(devices, depth, planes, width)
        received = exchange(back, None if part == 0 else (received, layers[: part - 1]))
        if part == 2:
            received, outputs = lax.optimization_barrier((received, outputs))
        field, low_x, high_x, low_y, high_y = z_inverse(received)
        halos = (
            shifted(high_x, "slab", 1),
            shifted(low_x, "slab", -1),
            shifted(high_y, "pen", 1),
            shifted(low_y, "pen", -1),
        )
        layers.append(halos)
        outputs = stretch(part, vorticity, field, halos, outputs)
    return (vorticity, outputs[0], outputs[1])


def solution(mesh):
    in_specs = (
        P("slab", "pen"),
        P("slab", "pen", None),
        P("slab", "pen", None),
        P(None, "slab", "pen", None),
        P(None, "slab", "pen", None),
    )
    out_specs = (
        P(None, "slab", "pen", None),
        P(None, "slab", "pen", None),
        P(None, "slab", "pen", None),
    )
    return jax.shard_map(
        per_device, mesh=mesh, in_specs=in_specs, out_specs=out_specs, check_vma=False
    )
```

```python
import functools
import math

import jax
import jax.numpy as jnp
import numpy as np
from jax import lax
from jax.experimental import pallas as pl
from jax.experimental.pallas import tpu as pltpu
from jax.sharding import PartitionSpec as P

NZ = 256
BLOCK_ROWS = 16
HALF = NZ // 2
STEP = 8
SLOTS_AT_ONCE = 256
MIB = 1024 * 1024
NEW = object()
AXES = ("slab", "pen")


def kernel_weight(distance):
    magnitude = jnp.abs(distance)
    inner_part = 1.0 - 2.5 * magnitude * magnitude + 1.5 * magnitude * magnitude * magnitude
    outer_part = 0.5 * (2.0 - magnitude) * (2.0 - magnitude) * (1.0 - magnitude)
    return jnp.where(magnitude < 1.0, inner_part, jnp.where(magnitude < 2.0, outer_part, 0.0))


def vmem(limit=48, **extra):
    return pltpu.CompilerParams(vmem_limit_bytes=limit * MIB, **extra)


def cost(flops, moved):
    return pl.CostEstimate(flops=int(flops), bytes_accessed=int(moved), transcendentals=0)


def two_parts(table):
    table = np.asarray(table, np.float32)
    high = table.astype(jnp.bfloat16)
    low = (table - high.astype(np.float32)).astype(jnp.bfloat16)
    return high, low


def right_table(table):
    high, low = two_parts(table)
    return jnp.asarray(np.concatenate([high, high, low], axis=0))


def left_table(table):
    high, low = two_parts(table)
    return jnp.asarray(np.concatenate([high, high, low], axis=1))


def waves(length):
    index = np.arange(length)
    angle = 2.0 * np.pi / length * (index[:, None] * index[None, :] % length)
    return np.cos(angle), np.sin(angle)


def z_forward_table():
    cosine, sine = waves(NZ)
    real_part, imaginary = cosine[:, :HALF].copy(), -sine[:, :HALF]
    imaginary[:, 0] = cosine[:, HALF]
    return np.concatenate([real_part, imaginary], axis=1)


def z_inverse_table():
    cosine, sine = waves(NZ)
    real_part, imaginary = 2.0 * cosine[:HALF], -2.0 * sine[:HALF]
    real_part[0] = 1.0
    imaginary[0] = cosine[HALF]
    return np.concatenate([real_part, imaginary], axis=0)


def y_forward_table(length, parts):
    cosine, sine = waves(length)
    width = length // parts
    rows = []
    for part in range(parts):
        here = slice(part * width, (part + 1) * width)
        rows.append(np.concatenate([cosine[here], -sine[here]], axis=1))
        rows.append(np.concatenate([sine[here], cosine[here]], axis=1))
    return np.concatenate(rows, axis=0)


def y_inverse_table(length, parts):
    cosine, sine = waves(length)
    width = length // parts
    columns = []
    for part in range(parts):
        here = slice(part * width, (part + 1) * width)
        columns.append(np.concatenate([cosine[:, here], -sine[:, here]], axis=0))
        columns.append(np.concatenate([sine[:, here], cosine[:, here]], axis=0))
    return np.concatenate(columns, axis=1)


def x_table(length, sign):
    cosine, sine = waves(length)
    return np.concatenate(
        [
            np.concatenate([cosine, -sign * sine], axis=1),
            np.concatenate([sign * sine, cosine], axis=1),
        ],
        axis=0,
    )


def split_values(values):
    high = values.astype(jnp.bfloat16)
    low = (values - high.astype(jnp.float32)).astype(jnp.bfloat16)
    return high, low


def times_right(values, table):
    high, low = split_values(values)
    return jnp.dot(
        jnp.concatenate([high, low, high], axis=1), table, preferred_element_type=jnp.float32
    )


def times_left(table, values):
    high, low = split_values(values)
    return jnp.dot(
        table, jnp.concatenate([high, low, high], axis=0), preferred_element_type=jnp.float32
    )


def deposit_kernel(begin, end, counts, row_base, z_base, fractions, strength, *refs):
    planes, blocks, slots = row_base.shape
    first_source = max(begin - 3, 0)
    last = end == planes
    width = min(SLOTS_AT_ONCE, slots)
    rows_local = blocks * BLOCK_ROWS
    ext = BLOCK_ROWS + 8
    if last:
        grid, ghost_y, ghost_x, ghost_xy = refs[:4]
    else:
        grid, ghost_y = refs[:2]
    rows, row_here, z_here, fractions_here, strength_here, arrived = refs[-6:]
    taken = slice(first_source, end)
    copies = [
        pltpu.make_async_copy(row_base.at[taken], row_here, arrived.at[0]),
        pltpu.make_async_copy(z_base.at[taken], z_here, arrived.at[1]),
        pltpu.make_async_copy(fractions.at[:, taken], fractions_here, arrived.at[2]),
        pltpu.make_async_copy(strength.at[:, taken], strength_here, arrived.at[3]),
    ]
    for copy in copies:
        copy.start()

    def clear(plane, _):
        grid[:, plane] = jnp.zeros((3,) + grid.shape[2:], jnp.float32)
        return 0

    lax.fori_loop(0, grid.shape[1], clear, 0)
    z_rows = 16
    z_iota = lax.broadcasted_iota(jnp.int32, (z_rows, width), 0)
    j_iota = lax.broadcasted_iota(jnp.int32, (ext, width), 0).astype(jnp.float32)
    z_tiles = [
        (z_iota + z_rows * t).astype(jnp.float32).astype(jnp.bfloat16) for t in range(NZ // z_rows)
    ]
    for copy in copies:
        copy.wait()

    def one_plane(offsets, source, _):
        plane = source + first_source
        slot = lax.broadcasted_iota(jnp.int32, (blocks, slots), 1)
        group = lax.broadcasted_iota(jnp.int32, (blocks, slots), 0)
        count = jnp.zeros((blocks, slots), jnp.int32)
        for block in range(blocks):
            count = jnp.where(group == block, counts[plane, block], count)
        live = slot < count
        row_cell = row_here[source].astype(jnp.float32)
        z_cell = z_here[source]
        for offset in range(4):
            weight_x = kernel_weight(float(offset - 1) - fractions_here[0, source])
            for part in range(3):
                rows[part * 4 + offset] = jnp.where(live, strength_here[part, source] * weight_x, 0.0)
            rows[12 + offset] = kernel_weight(float(offset - 1) - fractions_here[1, source])
            rows[16 + offset] = row_cell + float(offset)
            rows[20 + offset] = kernel_weight(float(offset - 1) - fractions_here[2, source])
            rows[24 + offset] = jnp.bitwise_and(z_cell + offset, NZ - 1).astype(jnp.float32)

        used = [(part, offset) for part in range(3) for offset in offsets]

        def spread(block, first):
            here = slice(first, first + width)

            def row(index):
                return rows[index, block : block + 1, here]

            weight_y = jnp.zeros((ext, width), jnp.float32)
            for offset in range(4):
                weight_y = jnp.where(j_iota == row(16 + offset), row(12 + offset), weight_y)
            coefs = jnp.concatenate([row(p * 4 + o) * weight_y for p, o in used], axis=0)
            coefs = coefs.astype(jnp.bfloat16)
            z_weight = [
                jnp.broadcast_to(row(20 + offset), (z_rows, width)).astype(jnp.bfloat16)
                for offset in range(4)
            ]
            z_place = [
                jnp.broadcast_to(row(24 + offset), (z_rows, width)).astype(jnp.bfloat16)
                for offset in range(4)
            ]
            tiles = []
            for z_tile in z_tiles:
                tile = jnp.zeros((z_rows, width), jnp.bfloat16)
                for offset in range(4):
                    tile = jnp.where(z_tile == z_place[offset], z_weight[offset], tile)
                tiles.append(tile)
            weight_z = jnp.concatenate(tiles, axis=0)
            result = lax.dot_general(
                coefs, weight_z, (((1,), (1,)), ((), ())), preferred_element_type=jnp.float32
            )
            low = block * BLOCK_ROWS
            for index, (part, offset) in enumerate(used):
                grid[part, plane + offset - begin, low : low + ext, :] += result[
                    index * ext : (index + 1) * ext
                ]

        for block in range(blocks):
            spread(block, 0)
        for first in range(width, slots, width):
            for block in range(blocks):
                pl.when(counts[plane, block] > first)(functools.partial(spread, block, first))
        return 0

    top = end + 3 if last else end
    inner_begin, inner_end = begin, top - 3
    for plane in range(first_source, begin):
        offsets = [o for o in range(4) if begin <= plane + o]
        one_plane(offsets, plane - first_source, 0)
    lax.fori_loop(
        inner_begin - first_source,
        inner_end - first_source,
        functools.partial(one_plane, list(range(4))),
        0,
    )
    for plane in range(inner_end, end):
        offsets = [o for o in range(4) if plane + o < top]
        one_plane(offsets, plane - first_source, 0)

    def side(plane, _):
        ghost_y[:, plane] = grid[:, plane, rows_local : rows_local + 3, :]
        return 0

    lax.fori_loop(0, end - begin, side, 0)
    if last:
        for part in range(3):
            for offset in range(3):
                plane = end - begin + offset
                ghost_x[part, offset] = grid[part, plane, :rows_local, :]
                ghost_xy[part, offset] = grid[part, plane, rows_local : rows_local + 3, :]


def deposit(particles, begin, end):
    planes, blocks, slots = particles[1].shape
    sources = end - max(begin - 3, 0)
    rows_local = blocks * BLOCK_ROWS
    whole = pl.BlockSpec(memory_space=pltpu.VMEM)
    last = end == planes
    shapes = [(3, end - begin + (3 if last else 0), rows_local + 8, NZ), (3, end - begin, 3, NZ)]
    if last:
        shapes += [(3, 3, rows_local, NZ), (3, 3, 3, NZ)]
    return pl.pallas_call(
        functools.partial(deposit_kernel, begin, end),
        out_shape=[jax.ShapeDtypeStruct(shape, jnp.float32) for shape in shapes],
        in_specs=[pl.BlockSpec(memory_space=pltpu.SMEM)]
        + [pl.BlockSpec(memory_space=pltpu.HBM)] * 4,
        out_specs=[whole] * len(shapes),
        scratch_shapes=[
            pltpu.VMEM((28, blocks, slots), jnp.float32),
            pltpu.VMEM((sources, blocks, slots), jnp.int32),
            pltpu.VMEM((sources, blocks, slots), jnp.int32),
            pltpu.VMEM((3, sources, blocks, slots), jnp.float32),
            pltpu.VMEM((3, sources, blocks, slots), jnp.float32),
            pltpu.SemaphoreType.DMA((4,)),
        ],
        compiler_params=vmem(60),
        cost_estimate=cost(10 * sources * blocks * 288 * slots * NZ, 12 * MIB),
        name="deposit",
    )(*particles)


def next_over(block, axes):
    counts = [lax.axis_size(axis) for axis in AXES]
    route = []
    for slab in range(counts[0]):
        for pen in range(counts[1]):
            to_slab = (slab + 1) % counts[0] if "slab" in axes else slab
            to_pen = (pen + 1) % counts[1] if "pen" in axes else pen
            route.append((slab * counts[1] + pen, to_slab * counts[1] + to_pen))
    return lax.ppermute(block, AXES, route)


def shifted(block, axis, distance):
    count = lax.axis_size(axis)
    return lax.ppermute(block, axis, [(i, (i + distance) % count) for i in range(count)])


def z_forward_body(with_x, grid, ghost_y, *refs):
    vorticity, send = refs[-2:]
    table = refs[-3]
    rows_local = vorticity.shape[2]
    vorticity[0] = grid[0, :, :rows_local, :]
    vorticity[0, :, 0:3, :] += ghost_y[0]
    if with_x:
        ghost_x, ghost_xy = refs[:2]

        @pl.when(pl.program_id(1) == 0)
        def _():
            vorticity[0, 0:3] += ghost_x[0]
            vorticity[0, 0:3, 0:3, :] += ghost_xy[0]

    spectrum = times_right(vorticity[0].reshape(STEP * rows_local, NZ), table[...])
    lines = send.reshape(HALF * STEP, 2 * rows_local)
    for plane in range(STEP):
        here = spectrum[plane * rows_local : (plane + 1) * rows_local]
        stacked = jnp.concatenate([here[:, :HALF], here[:, HALF:]], axis=0)
        lines[pl.ds(plane, HALF, stride=STEP), :] = stacked.T


def z_forward(parts, cell_range, deposited, ghosts_x, vorticity, send, shape):
    devices, depth, planes, width = shape
    begin, end = cell_range
    grid, ghost_y = deposited
    rows_local = width // 2
    count = len(parts)
    part = parts[0]
    table = right_table(z_forward_table())
    here = (end - begin) // STEP
    at = begin // STEP
    joined = send is not None
    send_at = at if joined else 0
    send_planes = planes if joined else end - begin
    specs = [
        pl.BlockSpec((1, STEP, rows_local + 8, NZ), lambda c, i: (part + c, i, 0, 0)),
        pl.BlockSpec((1, STEP, 3, NZ), lambda c, i: (part + c, i, 0, 0)),
    ]
    operands = [grid, ghost_y]
    if ghosts_x is not None:
        operands += list(ghosts_x)
        specs += [
            pl.BlockSpec((1, 3, rows_local, NZ), lambda c, i: (part + c, 0, 0, 0)),
            pl.BlockSpec((1, 3, 3, NZ), lambda c, i: (part + c, 0, 0, 0)),
        ]
    operands.append(table)
    specs.append(pl.BlockSpec(table.shape, lambda c, i: (0, 0)))
    aliases = {}
    for index, output in enumerate((vorticity, send)):
        if output is not None and output is not NEW:
            aliases[len(operands)] = index
            specs.append(pl.BlockSpec(memory_space=pl.ANY))
            operands.append(output)
    used = 5 if ghosts_x is not None else 3

    def kernel(*refs):
        z_forward_body(ghosts_x is not None, *refs[:used], *refs[-2:])

    return pl.pallas_call(
        kernel,
        grid=(count, here),
        in_specs=specs,
        out_specs=(
            pl.BlockSpec((1, STEP, rows_local, NZ), lambda c, i: (part + c, at + i, 0, 0)),
            pl.BlockSpec(
                (devices, None, depth, STEP, width), lambda c, i: (0, c, 0, send_at + i, 0)
            ),
        ),
        out_shape=(
            jax.ShapeDtypeStruct((3, planes, rows_local, NZ), jnp.float32),
            jax.ShapeDtypeStruct((devices, count, depth, send_planes, width), jnp.float32),
        ),
        input_output_aliases=aliases,
        compiler_params=vmem(),
        cost_estimate=cost(
            6 * count * here * STEP * rows_local * NZ * NZ,
            3 * count * here * STEP * rows_local * NZ * 4,
        ),
        name="z_forward",
    )(*operands)


def z_inverse_kernel(received, table, field, low_x, high_x, low_y, high_y):
    rows_local = field.shape[1]
    lines = received.reshape(HALF * STEP, 2 * rows_local)
    pieces = []
    for plane in range(STEP):
        turned = lines[pl.ds(plane, HALF, stride=STEP), :].T
        pieces.append(jnp.concatenate([turned[:rows_local], turned[rows_local:]], axis=1))
    values = times_right(jnp.concatenate(pieces, axis=0), table[...])
    field[...] = values.reshape(STEP, rows_local, NZ)
    low_y[...] = field[:, 0:2, :]
    high_y[...] = field[:, rows_local - 2 : rows_local, :]

    @pl.when(pl.program_id(0) == 0)
    def _():
        low_x[...] = field[0:2]

    @pl.when(pl.program_id(0) == pl.num_programs(0) - 1)
    def _():
        high_x[...] = field[STEP - 2 : STEP]


def z_inverse(received):
    devices, depth, planes, width = received.shape
    rows_local = width // 2
    table = right_table(z_inverse_table())
    layer = pl.BlockSpec((2, rows_local, NZ), lambda i: (0, 0, 0))
    edge = pl.BlockSpec((STEP, 2, NZ), lambda i: (i, 0, 0))
    return pl.pallas_call(
        z_inverse_kernel,
        grid=(planes // STEP,),
        in_specs=[
            pl.BlockSpec((devices, depth, STEP, width), lambda i: (0, 0, i, 0)),
            pl.BlockSpec(table.shape, lambda i: (0, 0)),
        ],
        out_specs=(
            pl.BlockSpec((STEP, rows_local, NZ), lambda i: (i, 0, 0)),
            layer,
            layer,
            edge,
            edge,
        ),
        out_shape=(
            jax.ShapeDtypeStruct((planes, rows_local, NZ), jnp.float32),
            jax.ShapeDtypeStruct((2, rows_local, NZ), jnp.float32),
            jax.ShapeDtypeStruct((2, rows_local, NZ), jnp.float32),
            jax.ShapeDtypeStruct((planes, 2, NZ), jnp.float32),
            jax.ShapeDtypeStruct((planes, 2, NZ), jnp.float32),
        ),
        compiler_params=vmem(),
        cost_estimate=cost(
            6 * planes * rows_local * NZ * NZ, 2 * planes * rows_local * NZ * 4
        ),
        name="z_inverse",
    )(received, table)


def plane_forward_kernel(start, *refs):
    y_table, x_table_ref, spectrum = refs[-3:]
    received = refs[:-3]
    step = pl.program_id(1)
    depth = pl.num_programs(1) - 1
    has_first = start[0] == 0

    @pl.when(jnp.logical_or(step < depth, has_first))
    def _():
        slabs, pens, _, width = received[0].shape
        pieces = []
        for pen in range(pens):
            piece = jnp.concatenate([cells[:, pen] for cells in received], axis=1)
            pieces.append(piece.reshape(slabs * piece.shape[1], width))
        lane = lax.broadcasted_iota(jnp.int32, (1, width), 1)
        real_side = lane < width // 2
        keep_real = jnp.logical_or(real_side, jnp.logical_not(jnp.logical_and(has_first, step == 0)))
        keep_imaginary = jnp.logical_or(jnp.logical_not(real_side), step < depth)
        keep = jnp.logical_and(keep_real, keep_imaginary).astype(jnp.float32)
        lines = jnp.concatenate([piece * keep for piece in pieces], axis=1)
        along_y = times_right(lines, y_table[...])
        rows_y = along_y.shape[1] // 2
        stacked = jnp.concatenate([along_y[:, :rows_y], along_y[:, rows_y:]], axis=0)
        spectrum[...] = times_left(x_table_ref[...], stacked)


def plane_forward(start, received):
    slabs, pens, count, depth, _, width = received[0].shape
    size_x = slabs * sum(cells.shape[4] for cells in received)
    size_y = pens * (width // 2)
    y_table = right_table(y_forward_table(size_y, pens))
    x_matrix = left_table(x_table(size_x, -1.0))
    return pl.pallas_call(
        plane_forward_kernel,
        grid=(count, depth + 1),
        in_specs=[pl.BlockSpec(memory_space=pltpu.SMEM)]
        + [
            pl.BlockSpec(
                (slabs, pens, None, None, cells.shape[4], width),
                lambda c, j: (0, 0, c, jnp.where(j < depth, j, 0), 0, 0),
            )
            for cells in received
        ]
        + [
            pl.BlockSpec(y_table.shape, lambda c, j: (0, 0)),
            pl.BlockSpec(x_matrix.shape, lambda c, j: (0, 0)),
        ],
        out_specs=pl.BlockSpec((None, None, 2 * size_x, size_y), lambda c, j: (c, j, 0, 0)),
        out_shape=jax.ShapeDtypeStruct((count, depth + 1, 2 * size_x, size_y), jnp.float32),
        compiler_params=vmem(),
        cost_estimate=cost(
            24 * count * depth * size_x * size_y * (size_x + size_y),
            4 * count * depth * size_x * size_y * 4,
        ),
        name="plane_forward",
    )(start, *received, y_table, x_matrix)


def wave_pair(shape, dim, length):
    index = lax.broadcasted_iota(jnp.int32, shape, dim)
    signed_index = jnp.where(index < length // 2, index, index - length)
    full_wave = (2.0 * math.pi / length) * signed_index.astype(jnp.float32)
    return full_wave, jnp.where(index == length // 2, 0.0, full_wave)


def plane_inverse_kernel(parts, needs, start, *refs):
    spectra = dict(zip(needs, refs[: len(needs)]))
    extras = dict(zip(needs, refs[len(needs) : 2 * len(needs)]))
    y_table, x_table_ref = refs[2 * len(needs) : 2 * len(needs) + 2]
    backs, turned = refs[2 * len(needs) + 2 : -1], refs[-1]
    step = pl.program_id(0)
    size_x, size_y = turned.shape[1] // 2, turned.shape[2]
    full_x, curl_x = wave_pair((size_x, 1), 0, size_x)
    full_y, curl_y = wave_pair((1, size_y), 1, size_y)

    def curl(part, source, full_z, curl_z):
        curls = (curl_x, curl_y, curl_z)
        wave_left, wave_right = curls[(part + 1) % 3], curls[(part + 2) % 3]
        left, right = source[(part + 1) % 3], source[(part + 2) % 3]
        wave_squared = full_x * full_x + full_y * full_y + full_z * full_z
        present = wave_squared > 0.0
        scaling = jnp.where(present, 1.0 / jnp.where(present, wave_squared, 1.0), 0.0)
        scaling = scaling * (1.0 / float(size_x * size_y * NZ))
        real_part = wave_left * right[:size_x] - wave_right * left[:size_x]
        imaginary = wave_left * right[size_x:] - wave_right * left[size_x:]
        return -imaginary * scaling, real_part * scaling

    index_z = (start[0] + step).astype(jnp.float32)
    wave_z = (2.0 * math.pi / NZ) * index_z
    for at, part in enumerate(parts):
        real_part, imaginary = curl(part, spectra, wave_z, wave_z)
        turned[at, :size_x] = real_part
        turned[at, size_x:] = imaginary

    @pl.when(jnp.logical_and(start[0] == 0, step == 0))
    def _():
        for at, part in enumerate(parts):
            extra_real, extra_imaginary = curl(part, extras, -math.pi, 0.0)
            turned[at, :size_x] += extra_real
            turned[at, size_x:] += extra_imaginary

    slabs, pens, planes, width = backs[0].shape
    for at, back in enumerate(backs):
        along_x = times_left(x_table_ref[...], turned[at])
        lines = jnp.concatenate([along_x[:size_x], along_x[size_x:]], axis=1)
        result = times_right(lines, y_table[...])
        for pen in range(pens):
            piece = result[:, pen * width : (pen + 1) * width]
            back[:, pen] = piece.reshape(slabs, planes, width)


def plane_inverse(parts, start, spectra, shape):
    slabs, pens, depth, planes, width = shape
    count = len(parts)
    size_x = slabs * planes
    size_y = pens * (width // 2)
    y_table = right_table(y_inverse_table(size_y, pens))
    x_matrix = left_table(x_table(size_x, 1.0))
    needs = [c for c in range(3) if any(c != part for part in parts)]

    def at(index, extra):
        return pl.BlockSpec(
            (None, None, 2 * size_x, size_y),
            lambda j: (index, depth if extra else j, 0, 0),
        )

    return pl.pallas_call(
        functools.partial(plane_inverse_kernel, parts, needs),
        grid=(depth,),
        in_specs=[pl.BlockSpec(memory_space=pltpu.SMEM)]
        + [at(spectra[c][1], False) for c in needs]
        + [at(spectra[c][1], True) for c in needs]
        + [
            pl.BlockSpec(y_table.shape, lambda j: (0, 0)),
            pl.BlockSpec(x_matrix.shape, lambda j: (0, 0)),
        ],
        out_specs=[
            pl.BlockSpec((slabs, pens, None, planes, width), lambda j: (0, 0, j, 0, 0))
        ]
        * count,
        out_shape=[jax.ShapeDtypeStruct(shape, jnp.float32)] * count,
        scratch_shapes=[pltpu.VMEM((count, 2 * size_x, size_y), jnp.float32)],
        compiler_params=vmem(),
        cost_estimate=cost(
            24 * count * depth * size_x * size_y * (size_x + size_y),
            6 * count * depth * size_x * size_y * 4,
        ),
        name="plane_inverse",
    )(start, *([spectra[c][0] for c in needs] * 2), y_table, x_matrix)


def z_difference_table():
    table = np.zeros((NZ, NZ), np.float32)
    for cell in range(NZ):
        for shift, weight in ((1, 8.0), (-1, -8.0), (2, -1.0), (-2, 1.0)):
            table[(cell + shift) % NZ, cell] += weight
    table = table.astype(jnp.bfloat16)
    return jnp.asarray(np.concatenate([table, table], axis=0))


def stretch_kernel(vorticity, field, before, after, low_x, high_x, low_y, high_y, table, *refs):
    velocity, stretching, padded = refs[-3:]
    step = pl.program_id(0)
    rows_local = field.shape[1]
    first = step == 0
    last = step == pl.num_programs(0) - 1
    own = slice(8, 8 + rows_local)
    for plane in range(STEP):
        padded[plane, own, :] = field[plane]
        padded[plane, 6:8, :] = low_y[plane]
        padded[plane, 8 + rows_local : 10 + rows_local, :] = high_y[plane]
    high, low = split_values(field[...].reshape(STEP * rows_local, NZ))
    along_z = jnp.dot(
        jnp.concatenate([high, low], axis=1), table[...], preferred_element_type=jnp.float32
    )

    def difference(ahead, behind, ahead_2, behind_2):
        return 8.0 * (ahead - behind) - (ahead_2 - behind_2)

    def along(plane):
        if plane < 0:
            return jnp.where(first, low_x[plane + 2], before[plane + 2])
        if plane >= STEP:
            return jnp.where(last, high_x[plane - STEP], after[plane - STEP])
        return field[plane]

    for plane in range(STEP):
        velocity[0, plane] = field[plane]
        along_x = difference(*(along(plane + shift) for shift in (1, -1, 2, -2)))
        along_y = difference(
            *(padded[plane, 8 + shift : 8 + shift + rows_local, :] for shift in (1, -1, 2, -2))
        )
        total = vorticity[0, plane] * along_x + vorticity[1, plane] * along_y
        total = total + vorticity[2, plane] * along_z[plane * rows_local : (plane + 1) * rows_local]
        stretching[0, plane] = total * (1.0 / 12.0)


def stretch(part, vorticity, field, halos, outputs):
    planes, rows_local, _ = field.shape
    pairs = STEP // 2
    table = z_difference_table()
    layer = pl.BlockSpec((2, rows_local, NZ), lambda i: (0, 0, 0))
    edge = pl.BlockSpec((STEP, 2, NZ), lambda i: (i, 0, 0))
    block = pl.BlockSpec((1, STEP, rows_local, NZ), lambda i: (part, i, 0, 0))
    specs = [
        pl.BlockSpec((3, STEP, rows_local, NZ), lambda i: (0, i, 0, 0)),
        pl.BlockSpec((STEP, rows_local, NZ), lambda i: (i, 0, 0)),
        pl.BlockSpec((2, rows_local, NZ), lambda i: (jnp.maximum(i * pairs - 1, 0), 0, 0)),
        pl.BlockSpec(
            (2, rows_local, NZ), lambda i: (jnp.minimum((i + 1) * pairs, planes // 2 - 1), 0, 0)
        ),
        layer,
        layer,
        edge,
        edge,
        pl.BlockSpec(table.shape, lambda i: (0, 0)),
    ]
    operands = [vorticity, field, field, field, *halos, table]
    aliases = {}
    if outputs is not None:
        aliases = {len(operands): 0, len(operands) + 1: 1}
        specs += [pl.BlockSpec(memory_space=pl.ANY)] * 2
        operands += list(outputs)
    shape = jax.ShapeDtypeStruct((3, planes, rows_local, NZ), jnp.float32)
    return pl.pallas_call(
        stretch_kernel,
        grid=(planes // STEP,),
        in_specs=specs,
        out_specs=(block, block),
        out_shape=(shape, shape),
        input_output_aliases=aliases,
        scratch_shapes=[pltpu.VMEM((STEP, rows_local + 16, NZ), jnp.float32)],
        compiler_params=vmem(),
        cost_estimate=cost(600 * planes * rows_local * NZ, 7 * planes * rows_local * NZ * 4),
        name="stretch",
    )(*operands)


def per_device(counts, row_base, z_base, fractions, strength):
    slabs, pens = lax.axis_size("slab"), lax.axis_size("pen")
    devices = slabs * pens
    depth = HALF // devices
    planes, blocks, _ = row_base.shape
    rows_local = blocks * BLOCK_ROWS
    width = 2 * rows_local
    place = lax.axis_index("slab") * pens + lax.axis_index("pen")
    start = (place * depth).astype(jnp.int32).reshape(1)
    shape = (devices, depth, planes, width)

    def exchange(blocks_out, after=None):
        if after is not None:
            blocks_out, _ = lax.optimization_barrier((blocks_out, after))
        return lax.all_to_all(blocks_out, AXES, 0, 0, tiled=True)

    def unfold(received):
        return received.reshape((slabs, pens) + received.shape[1:])

    cut = planes - STEP
    particles = (counts, row_base, z_base, fractions, strength)
    grid, ghost_y, ghost_x, ghost_xy = deposit(particles, cut, planes)
    tail = (grid, next_over(ghost_y, ("pen",)))
    ghosts_x = (next_over(ghost_x, ("slab",)), next_over(ghost_xy, ("slab", "pen")))
    everything = (cut, planes)
    if cut == 0:
        vorticity, send = z_forward((1, 2), everything, tail, ghosts_x, None, None, shape)
        received = [exchange(send)]
        vorticity, send = z_forward((0,), everything, tail, ghosts_x, vorticity, None, shape)
    else:
        vorticity, send = z_forward((1, 2), everything, tail, None, None, None, shape)
        held, _ = lax.optimization_barrier((particles, send))
        grid, ghost_y = deposit(held, 0, cut)
        head = (grid, next_over(ghost_y, ("pen",)))
        received = [exchange(send)]
        vorticity, send = z_forward((1, 2), (0, cut), head, ghosts_x, vorticity, None, shape)
        received = [exchange(send, received[0])] + received
        vorticity, send = z_forward((0,), (0, cut), head, ghosts_x, vorticity, NEW, shape)
        vorticity, send = z_forward((0,), everything, tail, None, vorticity, send, shape)
    pair = plane_forward(start, [unfold(cells) for cells in received])
    single = plane_forward(start, [unfold(exchange(send, received[0]))])
    spectra = {1: (pair, 0), 2: (pair, 1), 0: (single, 0)}

    shape = (slabs, pens, depth, planes, width)
    backs = plane_inverse((0,), start, spectra, shape) + plane_inverse((1, 2), start, spectra, shape)
    outputs = received = None
    layers = []
    for part, back in enumerate(backs):
        back = back.reshape(devices, depth, planes, width)
        received = exchange(back, None if part == 0 else (received, layers[: part - 1]))
        if part == 2:
            received, outputs = lax.optimization_barrier((received, outputs))
        field, low_x, high_x, low_y, high_y = z_inverse(received)
        halos = (
            shifted(high_x, "slab", 1),
            shifted(low_x, "slab", -1),
            shifted(high_y, "pen", 1),
            shifted(low_y, "pen", -1),
        )
        layers.append(halos)
        outputs = stretch(part, vorticity, field, halos, outputs)
    return (vorticity, outputs[0], outputs[1])


def solution(mesh):
    in_specs = (
        P("slab", "pen"),
        P("slab", "pen", None),
        P("slab", "pen", None),
        P(None, "slab", "pen", None),
        P(None, "slab", "pen", None),
    )
    out_specs = (
        P(None, "slab", "pen", None),
        P(None, "slab", "pen", None),
        P(None, "slab", "pen", None),
    )
    return jax.shard_map(
        per_device, mesh=mesh, in_specs=in_specs, out_specs=out_specs, check_vma=False
    )
```
